32 devices in a mesh: grp: 2 (over y), wide: 4 (over z), narrow: 4 (over x, core).
Axes of the slice: x: 2, y: 2, z: 4, core: 2. Of those that a mesh axis runs over, the one named last changes fastest.
Arguments:
- moe_input: bfloat16 [4096, 7168], P(('grp', 'wide', 'narrow')), parts along dimension 0, may hold values from -6 to 6
- expert_ids: int32 [4096, 8], P(('grp', 'wide', 'narrow')), parts along dimension 0, may hold values from 0 to 255, all different within a row; in each aligned block of 128 rows (0 to 127, 128 to 255, ...) at most 8 rows name the same one
- route_weights: float32 [4096, 8], P(('grp', 'wide', 'narrow')), parts along dimension 0, may hold values from 0.1 to 1
- expert_gate: bfloat16 [7168, 2048], P('wide', 'narrow'), may hold values from -0.0625 to 0.0625
- expert_up: bfloat16 [7168, 2048], P('wide', 'narrow'), may hold values from -0.0625 to 0.0625
- expert_down: bfloat16 [2048, 7168], P(None, ('wide', 'narrow')), may hold values from -0.125 to 0.125
Outputs:
- moe_output: bfloat16 [4096, 7168], P(('grp', 'wide', 'narrow')), parts along dimension 0
The draws below stay inside these ranges and needn't reach their ends.
There are 2 independent parts, one for each index of `grp`. The reference program is written for one: setup_inputs(seed, part) draws one part's arguments, and reference() takes and returns one part's arrays. A program takes and returns all parts, laid end to end along the dimension named above; an argument that names none is the same for every part. Nothing has to cross between parts.
Inputs may be any that keep to these rules, and one draw needn't show every extreme that they name: `expert_ids`: each row names 8 different experts. Among the 128 rows of one device (aligned blocks of 128 rows) no expert is named by more than 8 rows, a bound that some block reaches.
All inputs are finite; a program needn't handle non-finite values.
Results may differ from the reference program's by a relative error of at most 0.0058.
Values may be sent and summed in bfloat16 or wider, within the bound.
A program may use at most 64 MiB of HBM per device.

```python
import math
from functools import partial
import jax
import jax.numpy as jnp
import numpy as np
from jax import lax

D = 7168
FF = 2048
EXPERTS = 256
TOPK = 8
ROW_DEV = 128
CAP = 8
HOSTED = 1
M_ROWS = 2048


def steps_of(own_key, shape, shards, least, high):
    gain, own = 1.0, jax.random.fold_in(own_key, 6)
    for dim, blocks in shards:
        heights = jnp.exp(jax.random.uniform(jax.random.fold_in(own, dim), (blocks,), jnp.float32, least / len(shards), high / len(shards)))
        gain = gain * jnp.repeat(heights, shape[dim] // blocks).reshape([-1 if axis == dim else 1 for axis in range(len(shape))])
    return gain


def routed_block(stream_key, own, number, rows, amount, top, bound, skew):
    ranking = jax.random.permutation(stream_key, amount)
    packed, ordinary = portions_of(amount, rows * top, bound, skew, True), portions_of(amount, rows * top, bound, skew, False)
    places = jnp.arange(amount)

    def named(sizes, rotation):
        used = int((sizes > 0).sum())
        fixed = max(1, used // 4)
        shifted = fixed + (places - fixed + rotation * (used - fixed)) % max(1, amount - fixed)
        return jnp.zeros((amount,), jnp.int32).at[ranking[jnp.where(places < fixed, places, shifted)]].set(jnp.asarray(sizes, jnp.int32))

    sizes = jnp.where(number % 4 == 0, named(packed, number // 4), named(ordinary, number - number // 4 - 1))
    mixed = jax.random.permutation(jax.random.fold_in(own, 3), amount)
    giver, receiver = mixed[0:amount // 2 * 2:2], mixed[1:amount // 2 * 2:2]
    slack = jnp.minimum(sizes[giver] - 1, bound - sizes[receiver]) // 2
    slack = jnp.where((giver == ranking[0]) | (receiver == ranking[0]) | (sizes[receiver] == 0), 0, jnp.maximum(slack, 0))
    shifted = jax.random.randint(jax.random.fold_in(own, 4), (amount // 2,), 0, 1 << 20) % (slack + 1)
    sizes = sizes.at[giver].add(-shifted).at[receiver].add(shifted)
    members = jnp.searchsorted(jnp.cumsum(sizes), jnp.arange(rows * top), side="right").astype(jnp.int32)
    grid = members.reshape(top, rows).T
    grid = grid[jax.random.permutation(jax.random.fold_in(own, 1), rows)]
    rotation = jax.random.randint(jax.random.fold_in(own, 2), (rows, 1), 0, top)
    return jnp.take_along_axis(grid, (jnp.arange(top)[None, :] + rotation) % top, axis=1)


def portions_of(count, total, limit, lean, full):
    portions = [(1 << 20) // math.isqrt(grade ** lean) + 1 for grade in range(1, count + 1)]
    largest = limit if full else min(limit, max(-(-total // count), total * portions[0] // sum(portions)))
    least = 1 if total - largest >= count - 1 else 0
    holding, surplus = [largest] + [least] * (count - 1), total - largest - least * (count - 1)
    while surplus > 0:
        candidates = [i for i in range(1, count) if holding[i] < largest] or [i for i in range(1, count) if holding[i] < limit]
        mass, left = sum([portions[i] for i in candidates]), surplus
        for i in candidates:
            extra = min(limit - holding[i], max(1, left * portions[i] // mass), surplus)
            holding[i] = holding[i] + extra
            surplus = surplus - extra
    return np.array(holding)


def normal_values(rng, shape, width, most, split=(), kind=jnp.bfloat16):
    entries = jax.random.normal(rng, shape, jnp.float32) * width
    if len(split) > 0:
        entries = steps_of(rng, shape, split, -0.22, 0.18) * entries
    return jnp.clip(entries, min=-most, max=most).astype(kind)


def setup_inputs(seed: int = 0, part: int = 0) -> dict:
    seeds = jax.random.split(jax.random.key(seed), 7)
    part_splits = jax.random.split(jax.random.fold_in(seeds[6], part), 7)
    moe_input = normal_values(part_splits[0], (M_ROWS, D), 1.0, 6.0, ((0, 16),))
    expert_ids_keys = jax.random.split(jax.random.fold_in(part_splits[1], 1), M_ROWS // ROW_DEV)
    expert_ids_turns = jax.random.permutation(jax.random.fold_in(part_splits[1], 3), M_ROWS // ROW_DEV)
    expert_ids = jax.vmap(lambda own, number: routed_block(jax.random.fold_in(part_splits[1], 2), own, number, ROW_DEV, EXPERTS, TOPK, CAP, 2))(expert_ids_keys, expert_ids_turns).reshape((M_ROWS, TOPK))
    route_weights = jnp.clip(0.1 + 0.9 * jax.random.uniform(part_splits[2], (M_ROWS, TOPK), jnp.float32) ** steps_of(part_splits[2], (M_ROWS, TOPK), ((0, 16),), -0.2, 0.2), 0.1, 1.0)
    expert_gate = normal_values(seeds[3], (HOSTED * D, FF), D ** -0.5, 0.0625, ((0, 4), (1, 4)))
    expert_up = normal_values(seeds[4], (HOSTED * D, FF), D ** -0.5, 0.0625, ((0, 4), (1, 4)))
    expert_down = normal_values(seeds[5], (FF, HOSTED * D), FF ** -0.5, 0.125, ((1, 16),))
    return dict(moe_input=moe_input, expert_ids=expert_ids, route_weights=route_weights, expert_gate=expert_gate, expert_up=expert_up, expert_down=expert_down)


def expert_term(expert_index, running, x_blocks, id_blocks, weight_blocks, expert_gate, expert_up, expert_down):
    block_count = x_blocks.shape[0]
    matches = id_blocks == expert_index
    routed = jnp.any(matches, axis=-1).astype(jnp.int32)
    route_gain = jnp.sum(jnp.where(matches, weight_blocks, 0.0), axis=-1)
    slot_rank = jnp.cumsum(routed, axis=1) - routed
    selector = (slot_rank[:, None, :] == jnp.arange(CAP, dtype=jnp.int32)[None, :, None]) & (routed[:, None, :] > 0)
    slot_source = jnp.sum(jnp.where(selector, jnp.arange(ROW_DEV, dtype=jnp.int32)[None, None, :], 0), axis=-1).astype(jnp.int32)
    occupied = jnp.any(selector, axis=-1)
    gathered = jnp.take_along_axis(x_blocks, slot_source[:, :, None], axis=1)
    gathered = jnp.where(occupied[:, :, None], gathered, jnp.zeros_like(gathered)).reshape(block_count * CAP, D)
    start_row = (expert_index * D).astype(jnp.int32)
    gate_out = jnp.dot(gathered, lax.dynamic_slice_in_dim(expert_gate, start_row, D, 0), preferred_element_type=jnp.float32)
    up_out = jnp.dot(gathered, lax.dynamic_slice_in_dim(expert_up, start_row, D, 0), preferred_element_type=jnp.float32)
    hidden = (jax.nn.silu(gate_out) * up_out).astype(jnp.bfloat16)
    expert_out = jnp.dot(hidden, lax.dynamic_slice_in_dim(expert_down, start_row, D, 1), preferred_element_type=jnp.float32)
    expert_out = expert_out.astype(jnp.bfloat16).reshape(block_count, CAP, D)
    placed = jnp.einsum("bcr,bcd->brd", selector.astype(jnp.float32), expert_out.astype(jnp.float32), precision=lax.Precision.HIGHEST)
    return running + placed * route_gain[:, :, None]


def reference(moe_input, expert_ids, route_weights, expert_gate, expert_up, expert_down):
    block_count = M_ROWS // ROW_DEV
    x_blocks = moe_input.reshape(block_count, ROW_DEV, D)
    id_blocks = expert_ids.reshape(block_count, ROW_DEV, TOPK)
    weight_blocks = route_weights.reshape(block_count, ROW_DEV, TOPK)
    step_fn = partial(expert_term, x_blocks=x_blocks, id_blocks=id_blocks, weight_blocks=weight_blocks, expert_gate=expert_gate, expert_up=expert_up, expert_down=expert_down)
    start_total = jnp.zeros((block_count, ROW_DEV, D), jnp.float32)
    combined = lax.fori_loop(0, HOSTED, step_fn, start_total)
    return combined.reshape(M_ROWS, D).astype(jnp.bfloat16)
```

```python
import functools

import jax
import jax.numpy as jnp
from jax import lax
from jax.experimental import pallas as pl
from jax.experimental.pallas import tpu as pltpu
from jax.sharding import PartitionSpec as P

GROUP = 4
CAP = 8
MESH = pl.DeviceIdType.MESH
F32 = jnp.float32
BF16 = jnp.bfloat16


def slot_rows(ids):
    rows = ids.shape[0]
    hit = (ids == 0).astype(F32).astype(BF16)
    ones = jnp.ones((16, ids.shape[1]), BF16)
    routed = lax.dot_general(ones, hit, (((1,), (1,)), ((), ())), preferred_element_type=F32)
    before = lax.broadcasted_iota(jnp.int32, (rows, rows), 0) < lax.broadcasted_iota(jnp.int32, (rows, rows), 1)
    rank = jnp.dot(routed.astype(BF16), before.astype(F32).astype(BF16), preferred_element_type=F32)
    slot = lax.broadcasted_iota(jnp.int32, (16, rows), 0)
    slot = jnp.where(slot >= CAP, slot - CAP, slot).astype(F32)
    return jnp.where((rank == slot) & (routed > 0.5), 1.0, 0.0).astype(BF16)


def expert_kernel(
    ids_ref, x_hbm, gate_hbm, up_hbm, down_hbm, ret_ref,
    x_v, gu_v, down_v, xq, seg, lhs, pbuf, rs, own, hid, obuf, ret,
    x_sem, gu_sem, down_sem,
    a_send, a_recv, b_send, b_recv, c_send, c_recv,
    r_send, r_recv,
    ha_send, ha_recv, hb_send, hb_recv, hc_send, hc_recv,
    o_send, o_recv,
):
    w = lax.axis_index("wide")
    n = lax.axis_index("narrow")
    me = w * 4 + n
    mate = n + 1 - 2 * lax.rem(n, 2)
    across = lax.rem(n + 2, 4)
    diag = lax.rem(mate + 2, 4)
    quarter = gate_hbm.shape[0]
    half = quarter // 2
    block = gate_hbm.shape[1] // 4
    rows = lhs.shape[0]

    def ahead(k):
        return lax.rem(w + k, 4)

    def behind(k):
        return lax.rem(w + 4 - k, 4)

    loads_x = []
    for k in (2, 1, 3, 0):
        cols = pl.ds(pl.multiple_of(ahead(k) * quarter, 128), quarter)
        loads_x.append(pltpu.make_async_copy(x_hbm.at[:, cols], x_v.at[k], x_sem.at[k]))
    for copy in loads_x:
        copy.start()
    loads_gu = []
    for j in range(4):
        for half_no, src in ((0, gate_hbm), (1, up_hbm)):
            loads_gu.append(
                pltpu.make_async_copy(
                    src.at[:, pl.ds(j * block, block)],
                    gu_v.at[:, pl.ds((2 * j + half_no) * block, block)],
                    gu_sem.at[2 * j + half_no],
                )
            )
    for copy in loads_gu:
        copy.start()
    load_down = pltpu.make_async_copy(down_hbm, down_v, down_sem.at[0])
    load_down.start()

    barrier = pltpu.get_barrier_semaphore()
    for t in range(1, 16):
        d = lax.rem(me + t, 16)
        pl.semaphore_signal(
            barrier, inc=1, device_id={"wide": d // 4, "narrow": lax.rem(d, 4)}, device_id_type=MESH
        )

    pick = slot_rows(ids_ref[...])

    def gathered(k):
        first = jnp.dot(pick, x_v[k, :, :half], preferred_element_type=F32)
        second = jnp.dot(pick, x_v[k, :, half:], preferred_element_type=F32)
        return jnp.concatenate([first[:CAP], second[CAP:]], axis=0).astype(BF16)

    pl.semaphore_wait(barrier, 15)

    def remote(src, dst, send, recv, device):
        return pltpu.make_async_remote_copy(
            src_ref=src, dst_ref=dst, send_sem=send, recv_sem=recv, device_id=device, device_id_type=MESH
        )

    started = []

    def go(copy):
        copy.start()
        started.append(copy)
        return copy

    def spread(buf, place, a_copies, bs, br, cs, cr):
        cross = {}
        close = {}
        last = {}

        def forward(k):
            s = place(behind(k), n)
            close[k] = go(remote(buf.at[s], buf.at[s], bs.at[k], br.at[k], {"narrow": mate}))
            cross[k] = go(remote(buf.at[s], buf.at[s], bs.at[4 + k], br.at[4 + k], {"narrow": across}))

        def relay(k):
            cross[k].wait_recv()
            s = place(behind(k), across)
            last[k] = go(remote(buf.at[s], buf.at[s], cs.at[k], cr.at[k], {"narrow": mate}))

        forward(0)
        order = (0, 1, 3, 2)
        for i in range(1, 4):
            a_copies[order[i]].wait_recv()
            forward(order[i])
            relay(order[i - 1])
        relay(order[3])
        return close, last

    seg_place = lambda w_, n_: w_ * 4 + n_
    a_copies = {}
    for i, k in enumerate((2, 1, 3, 0)):
        loads_x[i].wait()
        value = gathered(k)
        if k:
            xq[k] = value
            a_copies[k] = go(
                remote(xq.at[k], seg.at[me], a_send.at[k], a_recv.at[k], {"wide": ahead(k)})
            )
        else:
            seg[me] = value
    close, last = spread(seg, seg_place, a_copies, b_send, b_recv, c_send, c_recv)
    for k in range(4):
        close[k].wait_recv()
    for k in range(4):
        last[k].wait_recv()
    for j in range(4):
        part = seg[4 * j:4 * j + 4].astype(F32)
        lhs[32 * j:32 * j + 32, :half] = part[:, :CAP].reshape(32, half).astype(BF16)
        lhs[32 * j:32 * j + 32, half:] = part[:, CAP:].reshape(32, half).astype(BF16)
    for copy in loads_gu:
        copy.wait()

    r_copies = {}
    for k in (2, 1, 3, 0):
        cols = pl.ds(pl.multiple_of(ahead(k) * 2 * block, 128), 2 * block)
        value = jnp.dot(lhs[...], gu_v[:, cols], preferred_element_type=F32)
        if k:
            pbuf[k] = value.astype(BF16)
            r_copies[k] = go(remote(pbuf.at[k], rs.at[k], r_send.at[k], r_recv.at[k], {"wide": ahead(k)}))
        else:
            own[...] = value
    for k in (1, 3, 2):
        r_copies[k].wait_recv()
    total = own[...] + rs[1].astype(F32) + rs[3].astype(F32) + rs[2].astype(F32)
    gate, up = total[:, :block], total[:, block:]
    mine = n * 4 + w
    hid[mine] = (gate / (1.0 + jnp.exp(-gate)) * up).astype(BF16)

    hid_place = lambda w_, n_: n_ * 4 + w_
    h_copies = {}
    for k in (2, 1, 3):
        h_copies[k] = go(
            remote(hid.at[mine], hid.at[mine], ha_send.at[k], ha_recv.at[k], {"wide": ahead(k)})
        )
    close, last = spread(hid, hid_place, h_copies, hb_send, hb_recv, hc_send, hc_recv)
    load_down.wait()

    def down_part(n_):
        left = jnp.concatenate([hid[n_ * 4 + j] for j in range(4)], axis=1)
        right = down_v[pl.ds(pl.multiple_of(n_ * 4 * block, 128), 4 * block), :]
        return jnp.dot(left, right, preferred_element_type=F32)

    out = down_part(n)
    out = out + down_part(across)
    for k in range(4):
        close[k].wait_recv()
    out = out + down_part(mate)
    for k in range(4):
        last[k].wait_recv()
    out = out + down_part(diag)

    width = out.shape[1]
    wide_half = obuf.shape[2]
    first = out[:, :wide_half].reshape(16, CAP, wide_half)
    second = jnp.concatenate(
        [out[:, wide_half:], jnp.zeros((rows, 2 * wide_half - width), F32)], axis=1
    ).reshape(16, CAP, wide_half)
    obuf[...] = jnp.concatenate([first, second], axis=1).astype(BF16)
    o_copies = []
    for t in range(1, 16):
        d = lax.rem(me + t, 16)
        o_copies.append(
            go(
                remote(
                    obuf.at[d], ret.at[me], o_send.at[t], o_recv.at[t],
                    {"wide": d // 4, "narrow": lax.rem(d, 4)},
                )
            )
        )
    ret[me] = obuf[me]
    for copy in o_copies:
        copy.wait_recv()
    ret_ref[...] = ret[...]
    for copy in started:
        copy.wait_send()


def combine_kernel(width, ids_ref, weights_ref, ret_ref, out_ref):
    ids = ids_ref[...]
    rows = ids.shape[0]
    hit = ids == 0
    gain = jnp.sum(jnp.where(hit, weights_ref[...], 0.0), axis=1, keepdims=True)
    routed = jnp.sum(jnp.where(hit, 1.0, 0.0), axis=1, keepdims=True)
    routed = jnp.broadcast_to(routed, (rows, 16))
    after = lax.broadcasted_iota(jnp.int32, (rows, rows), 0) > lax.broadcasted_iota(jnp.int32, (rows, rows), 1)
    rank = jnp.dot(after.astype(F32).astype(BF16), routed.astype(BF16), preferred_element_type=F32)
    slot = lax.broadcasted_iota(jnp.int32, (rows, 16), 1).astype(F32)
    place = jnp.where((rank == slot) & (routed > 0.5) & (slot < CAP), 1.0, 0.0).astype(BF16)
    pieces = []
    wide_half = ret_ref.shape[2]
    for j in range(ret_ref.shape[0]):
        value = ret_ref[j].astype(F32)
        pieces += [value[:CAP], value[CAP:, :width - wide_half]]
    slots = jnp.concatenate(pieces, axis=1)
    slots = jnp.concatenate([slots, jnp.zeros_like(slots)], axis=0).astype(BF16)
    out_ref[...] = (jnp.dot(place, slots, preferred_element_type=F32) * gain).astype(BF16)


def grouped(moe_input, expert_ids, route_weights, expert_gate, expert_up, expert_down):
    rows, model = moe_input.shape
    quarter, hidden = expert_gate.shape
    width = expert_down.shape[1]
    block = hidden // 4
    wide_half = -(-width // 256) * 128
    all_rows = 16 * CAP
    dma = pltpu.SemaphoreType.DMA
    any_spec = pl.BlockSpec(memory_space=pl.ANY)
    vmem_spec = pl.BlockSpec(memory_space=pltpu.VMEM)
    returned = pl.pallas_call(
        expert_kernel,
        out_shape=jax.ShapeDtypeStruct((16, 16, wide_half), BF16),
        in_specs=[vmem_spec] + [any_spec] * 4,
        out_specs=vmem_spec,
        scratch_shapes=[
            pltpu.VMEM((4, rows, quarter), BF16),
            pltpu.VMEM((quarter, 2 * hidden), BF16),
            pltpu.VMEM(expert_down.shape, BF16),
            pltpu.VMEM((4, 16, quarter // 2), BF16),
            pltpu.VMEM((16, 16, quarter // 2), BF16),
            pltpu.VMEM((all_rows, quarter), BF16),
            pltpu.VMEM((4, all_rows, 2 * block), BF16),
            pltpu.VMEM((4, all_rows, 2 * block), BF16),
            pltpu.VMEM((all_rows, 2 * block), F32),
            pltpu.VMEM((16, all_rows, block), BF16),
            pltpu.VMEM((16, 16, wide_half), BF16),
            pltpu.VMEM((16, 16, wide_half), BF16),
            dma((4,)), dma((8,)), dma((1,)),
            dma((4,)), dma((4,)), dma((8,)), dma((8,)), dma((4,)), dma((4,)),
            dma((4,)), dma((4,)),
            dma((4,)), dma((4,)), dma((8,)), dma((8,)), dma((4,)), dma((4,)),
            dma((16,)), dma((16,)),
        ],
        compiler_params=pltpu.CompilerParams(
            collective_id=0, has_side_effects=True, vmem_limit_bytes=56 * 1024 * 1024
        ),
    )(expert_ids, moe_input, expert_gate, expert_up, expert_down)
    parts = 4
    return pl.pallas_call(
        functools.partial(combine_kernel, width),
        out_shape=jax.ShapeDtypeStruct((rows, model), BF16),
        grid=(parts,),
        in_specs=[
            pl.BlockSpec(expert_ids.shape, lambda i: (0, 0)),
            pl.BlockSpec(route_weights.shape, lambda i: (0, 0)),
            pl.BlockSpec((16 // parts, 16, wide_half), lambda i: (i, 0, 0)),
        ],
        out_specs=pl.BlockSpec((rows, model // parts), lambda i: (0, i)),
    )(expert_ids, route_weights, returned)


def from_partner(block, axis, stride):
    count = lax.axis_size(axis)
    route = []
    for low in range(count):
        high = low | 1 << stride
        if high != low and high < count:
            route += [(low, high), (high, low)]
    return lax.ppermute(block, axis, route)


def shards(moe_input, expert_ids, route_weights, expert_gate, expert_up, expert_down):
    wide_count = lax.axis_size("wide")
    narrow_count = lax.axis_size("narrow")
    hosted = wide_count // GROUP
    row_count = moe_input.shape[0]
    quarter = moe_input.shape[1] // GROUP
    hidden_width = expert_gate.shape[1]
    out_cols = expert_down.shape[1]
    matches = expert_ids[:, :, None] == jnp.arange(hosted, dtype=jnp.int32)[None, None, :]
    routed = jnp.any(matches, axis=1).astype(jnp.int32)
    route_gain = jnp.sum(jnp.where(matches, route_weights[:, :, None], 0.0), axis=1)
    slot_rank = jnp.cumsum(routed, axis=0) - routed
    selector = (slot_rank.T[:, None, :] == jnp.arange(CAP, dtype=jnp.int32)[None, :, None]) & (
        routed.T[:, None, :] > 0
    )
    quarters = moe_input.reshape(row_count, GROUP, quarter)
    outgoing = jnp.einsum(
        "ecr,rqd->eqcd", selector.astype(jnp.bfloat16), quarters, preferred_element_type=jnp.float32
    )
    outgoing = outgoing.astype(jnp.bfloat16).reshape(hosted * GROUP, CAP, quarter)
    arrived = lax.all_to_all(outgoing, "wide", split_axis=0, concat_axis=1, tiled=True).reshape(
        wide_count * CAP, quarter
    )
    segment = lax.all_gather(arrived, "narrow", axis=0, tiled=True)
    gate_part = jnp.dot(segment, expert_gate, preferred_element_type=jnp.float32)
    up_part = jnp.dot(segment, expert_up, preferred_element_type=jnp.float32)
    partial_sums = jnp.concatenate([gate_part, up_part], axis=1)
    summed = partial_sums
    for level in range(2):
        summed = summed + from_partner(summed, "wide", level)
    hidden = (jax.nn.silu(summed[:, :hidden_width]) * summed[:, hidden_width:]).astype(jnp.bfloat16)
    expert_out = jnp.dot(
        lax.all_gather(hidden, "narrow", axis=1, tiled=True),
        expert_down,
        preferred_element_type=jnp.float32,
    ).astype(jnp.bfloat16)
    sectioned = expert_out.reshape(narrow_count, wide_count, CAP, 1, out_cols)
    returned = lax.all_to_all(
        lax.all_to_all(sectioned, "wide", split_axis=1, concat_axis=3, tiled=True),
        "narrow",
        split_axis=0,
        concat_axis=4,
        tiled=True,
    )
    returned = returned.reshape(CAP, hosted, GROUP * quarter)
    weighted = selector.astype(jnp.float32) * route_gain.T[:, None, :]
    combined = jnp.einsum(
        "ecr,ced->rd", weighted, returned.astype(jnp.float32), precision=lax.Precision.HIGHEST
    )
    return combined.astype(jnp.bfloat16)


def solution(mesh):
    in_specs = (
        P(("grp", "wide", "narrow"), None),
        P(("grp", "wide", "narrow"), None),
        P(("grp", "wide", "narrow"), None),
        P("wide", "narrow"),
        P("wide", "narrow"),
        P(None, ("wide", "narrow")),
    )
    out_specs = P(("grp", "wide", "narrow"), None)
    single = mesh.shape["wide"] == GROUP and mesh.shape["narrow"] == 4
    per_device = grouped if single else shards
    return jax.shard_map(per_device, mesh=mesh, in_specs=in_specs, out_specs=out_specs, check_vma=False)
```

```python
import functools

import jax
import jax.numpy as jnp
from jax import lax
from jax.experimental import pallas as pl
from jax.experimental.pallas import tpu as pltpu
from jax.sharding import PartitionSpec as P

GROUP = 4
CAP = 8
MESH = pl.DeviceIdType.MESH
F32 = jnp.float32
BF16 = jnp.bfloat16


def slot_rows(ids):
    rows = ids.shape[1]
    routed = jnp.sum(jnp.where(ids == 0, 1.0, 0.0), axis=0, keepdims=True)
    routed = jnp.broadcast_to(routed, (16, rows))
    before = lax.broadcasted_iota(jnp.int32, (rows, rows), 0) < lax.broadcasted_iota(jnp.int32, (rows, rows), 1)
    rank = jnp.dot(routed.astype(BF16), before.astype(F32).astype(BF16), preferred_element_type=F32)
    slot = lax.broadcasted_iota(jnp.int32, (16, rows), 0)
    slot = jnp.where(slot >= CAP, slot - CAP, slot).astype(F32)
    return jnp.where((rank == slot) & (routed > 0.5), 1.0, 0.0).astype(BF16)


def expert_kernel(
    ids_ref, x_hbm, gate_hbm, up_hbm, down_hbm, ret_ref,
    x_v, gu_v, down_v, xq, seg, lhs, pbuf, rs, own, hid, obuf, ret,
    x_sem, gu_sem, down_sem,
    a_send, a_recv, b_send, b_recv, c_send, c_recv,
    r_send, r_recv,
    ha_send, ha_recv, hb_send, hb_recv, hc_send, hc_recv,
    o_send, o_recv,
):
    w = lax.axis_index("wide")
    n = lax.axis_index("narrow")
    me = w * 4 + n
    mate = n + 1 - 2 * lax.rem(n, 2)
    across = lax.rem(n + 2, 4)
    diag = lax.rem(mate + 2, 4)
    quarter = gate_hbm.shape[0]
    half = quarter // 2
    block = gate_hbm.shape[1] // 4
    rows = lhs.shape[0]

    def ahead(k):
        return lax.rem(w + k, 4)

    def behind(k):
        return lax.rem(w + 4 - k, 4)

    loads_x = []
    for k in (2, 1, 3, 0):
        cols = pl.ds(pl.multiple_of(ahead(k) * quarter, 128), quarter)
        loads_x.append(pltpu.make_async_copy(x_hbm.at[:, cols], x_v.at[k], x_sem.at[k]))
    for copy in loads_x:
        copy.start()
    loads_gu = []
    for j in range(4):
        for half_no, src in ((0, gate_hbm), (1, up_hbm)):
            loads_gu.append(
                pltpu.make_async_copy(
                    src.at[:, pl.ds(j * block, block)],
                    gu_v.at[:, pl.ds((2 * j + half_no) * block, block)],
                    gu_sem.at[2 * j + half_no],
                )
            )
    for copy in loads_gu:
        copy.start()
    load_down = pltpu.make_async_copy(down_hbm, down_v, down_sem.at[0])
    load_down.start()

    barrier = pltpu.get_barrier_semaphore()
    for t in range(1, 16):
        d = lax.rem(me + t, 16)
        pl.semaphore_signal(
            barrier, inc=1, device_id={"wide": d // 4, "narrow": lax.rem(d, 4)}, device_id_type=MESH
        )

    pick = slot_rows(ids_ref[...])

    def gathered(k):
        first = jnp.dot(pick, x_v[k, :, :half], preferred_element_type=F32)
        second = jnp.dot(pick, x_v[k, :, half:], preferred_element_type=F32)
        return jnp.concatenate([first[:CAP], second[CAP:]], axis=0).astype(BF16)

    pl.semaphore_wait(barrier, 15)

    def remote(src, dst, send, recv, device):
        return pltpu.make_async_remote_copy(
            src_ref=src, dst_ref=dst, send_sem=send, recv_sem=recv, device_id=device, device_id_type=MESH
        )

    started = []

    def go(copy):
        copy.start()
        started.append(copy)
        return copy

    def spread(buf, place, a_copies, bs, br, cs, cr):
        cross = {}
        close = {}
        last = {}

        def forward(k):
            s = place(behind(k), n)
            close[k] = go(remote(buf.at[s], buf.at[s], bs.at[k], br.at[k], {"narrow": mate}))
            cross[k] = go(remote(buf.at[s], buf.at[s], bs.at[4 + k], br.at[4 + k], {"narrow": across}))

        def relay(k):
            cross[k].wait_recv()
            s = place(behind(k), across)
            last[k] = go(remote(buf.at[s], buf.at[s], cs.at[k], cr.at[k], {"narrow": mate}))

        forward(0)
        order = (0, 1, 3, 2)
        for i in range(1, 4):
            a_copies[order[i]].wait_recv()
            forward(order[i])
            relay(order[i - 1])
        relay(order[3])
        return close, last

    seg_place = lambda w_, n_: w_ * 4 + n_
    a_copies = {}
    for i, k in enumerate((2, 1, 3, 0)):
        loads_x[i].wait()
        value = gathered(k)
        if k:
            xq[k] = value
            a_copies[k] = go(
                remote(xq.at[k], seg.at[me], a_send.at[k], a_recv.at[k], {"wide": ahead(k)})
            )
        else:
            seg[me] = value
    close, last = spread(seg, seg_place, a_copies, b_send, b_recv, c_send, c_recv)
    for k in range(4):
        close[k].wait_recv()
    for k in range(4):
        last[k].wait_recv()
    for j in range(4):
        part = seg[4 * j:4 * j + 4].astype(F32)
        lhs[32 * j:32 * j + 32, :half] = part[:, :CAP].reshape(32, half).astype(BF16)
        lhs[32 * j:32 * j + 32, half:] = part[:, CAP:].reshape(32, half).astype(BF16)
    for copy in loads_gu:
        copy.wait()

    r_copies = {}
    for k in (2, 1, 3, 0):
        cols = pl.ds(pl.multiple_of(ahead(k) * 2 * block, 128), 2 * block)
        value = jnp.dot(lhs[...], gu_v[:, cols], preferred_element_type=F32)
        if k:
            pbuf[k] = value.astype(BF16)
            r_copies[k] = go(remote(pbuf.at[k], rs.at[k], r_send.at[k], r_recv.at[k], {"wide": ahead(k)}))
        else:
            own[...] = value
    for k in (1, 3, 2):
        r_copies[k].wait_recv()
    total = own[...] + rs[1].astype(F32) + rs[3].astype(F32) + rs[2].astype(F32)
    gate, up = total[:, :block], total[:, block:]
    mine = n * 4 + w
    hid[mine] = (gate / (1.0 + jnp.exp(-gate)) * up).astype(BF16)

    hid_place = lambda w_, n_: n_ * 4 + w_
    h_copies = {}
    for k in (2, 1, 3):
        h_copies[k] = go(
            remote(hid.at[mine], hid.at[mine], ha_send.at[k], ha_recv.at[k], {"wide": ahead(k)})
        )
    close, last = spread(hid, hid_place, h_copies, hb_send, hb_recv, hc_send, hc_recv)
    load_down.wait()

    def down_part(n_):
        left = jnp.concatenate([hid[n_ * 4 + j] for j in range(4)], axis=1)
        right = down_v[:, pl.ds(pl.multiple_of(n_ * 4 * block, 128), 4 * block)]
        return lax.dot_general(left, right, (((1,), (1,)), ((), ())), preferred_element_type=F32)

    out = down_part(n)
    out = out + down_part(across)
    for k in range(4):
        close[k].wait_recv()
    out = out + down_part(mate)
    for k in range(4):
        last[k].wait_recv()
    out = out + down_part(diag)

    width = out.shape[1]
    wide_half = obuf.shape[2]
    first = out[:, :wide_half].reshape(16, CAP, wide_half)
    second = jnp.concatenate(
        [out[:, wide_half:], jnp.zeros((rows, 2 * wide_half - width), F32)], axis=1
    ).reshape(16, CAP, wide_half)
    obuf[...] = jnp.concatenate([first, second], axis=1).astype(BF16)
    o_copies = []
    for t in range(1, 16):
        d = lax.rem(me + t, 16)
        o_copies.append(
            go(
                remote(
                    obuf.at[d], ret.at[me], o_send.at[t], o_recv.at[t],
                    {"wide": d // 4, "narrow": lax.rem(d, 4)},
                )
            )
        )
    ret[me] = obuf[me]
    for copy in o_copies:
        copy.wait_recv()
    ret_ref[...] = ret[...]
    for copy in started:
        copy.wait_send()


def combine_kernel(width, ids_ref, weights_ref, ret_ref, out_ref):
    ids = ids_ref[...]
    rows = ids.shape[1]
    hit = ids == 0
    gain = jnp.sum(jnp.where(hit, weights_ref[...], 0.0), axis=0, keepdims=True)
    gain = jnp.transpose(jnp.broadcast_to(gain, (128, rows)))
    place = slot_rows(ids)
    place = jnp.where(lax.broadcasted_iota(jnp.int32, place.shape, 0) < CAP, place.astype(F32), 0.0).astype(BF16)
    pieces = []
    wide_half = ret_ref.shape[2]
    for j in range(ret_ref.shape[0]):
        value = ret_ref[j].astype(F32)
        pieces += [value[:CAP], value[CAP:, :width - wide_half]]
    slots = jnp.concatenate(pieces, axis=1)
    slots = jnp.concatenate([slots, jnp.zeros_like(slots)], axis=0).astype(BF16)
    placed = lax.dot_general(place, slots, (((0,), (0,)), ((), ())), preferred_element_type=F32)
    gains = jnp.concatenate([gain] * (placed.shape[1] // 128), axis=1)
    out_ref[...] = (placed * gains).astype(BF16)


def grouped(moe_input, expert_ids, route_weights, expert_gate, expert_up, expert_down):
    rows, model = moe_input.shape
    quarter, hidden = expert_gate.shape
    width = expert_down.shape[1]
    block = hidden // 4
    wide_half = -(-width // 256) * 128
    all_rows = 16 * CAP
    ids, weights = expert_ids.T, route_weights.T
    dma = pltpu.SemaphoreType.DMA
    any_spec = pl.BlockSpec(memory_space=pl.ANY)
    vmem_spec = pl.BlockSpec(memory_space=pltpu.VMEM)
    returned = pl.pallas_call(
        expert_kernel,
        out_shape=jax.ShapeDtypeStruct((16, 16, wide_half), BF16),
        in_specs=[vmem_spec] + [any_spec] * 4,
        out_specs=vmem_spec,
        scratch_shapes=[
            pltpu.VMEM((4, rows, quarter), BF16),
            pltpu.VMEM((quarter, 2 * hidden), BF16),
            pltpu.VMEM(expert_down.shape[::-1], BF16),
            pltpu.VMEM((4, 16, quarter // 2), BF16),
            pltpu.VMEM((16, 16, quarter // 2), BF16),
            pltpu.VMEM((all_rows, quarter), BF16),
            pltpu.VMEM((4, all_rows, 2 * block), BF16),
            pltpu.VMEM((4, all_rows, 2 * block), BF16),
            pltpu.VMEM((all_rows, 2 * block), F32),
            pltpu.VMEM((16, all_rows, block), BF16),
            pltpu.VMEM((16, 16, wide_half), BF16),
            pltpu.VMEM((16, 16, wide_half), BF16),
            dma((4,)), dma((8,)), dma((1,)),
            dma((4,)), dma((4,)), dma((8,)), dma((8,)), dma((4,)), dma((4,)),
            dma((4,)), dma((4,)),
            dma((4,)), dma((4,)), dma((8,)), dma((8,)), dma((4,)), dma((4,)),
            dma((16,)), dma((16,)),
        ],
        compiler_params=pltpu.CompilerParams(
            collective_id=0, has_side_effects=True, vmem_limit_bytes=56 * 1024 * 1024
        ),
    )(ids, moe_input, expert_gate, expert_up, expert_down.T)
    parts = 4
    return pl.pallas_call(
        functools.partial(combine_kernel, width),
        out_shape=jax.ShapeDtypeStruct((rows, model), BF16),
        grid=(parts,),
        in_specs=[
            pl.BlockSpec(ids.shape, lambda i: (0, 0)),
            pl.BlockSpec(weights.shape, lambda i: (0, 0)),
            pl.BlockSpec((16 // parts, 16, wide_half), lambda i: (i, 0, 0)),
        ],
        out_specs=pl.BlockSpec((rows, model // parts), lambda i: (0, i)),
    )(ids, weights, returned)


def from_partner(block, axis, stride):
    count = lax.axis_size(axis)
    route = []
    for low in range(count):
        high = low | 1 << stride
        if high != low and high < count:
            route += [(low, high), (high, low)]
    return lax.ppermute(block, axis, route)


def shards(moe_input, expert_ids, route_weights, expert_gate, expert_up, expert_down):
    wide_count = lax.axis_size("wide")
    narrow_count = lax.axis_size("narrow")
    hosted = wide_count // GROUP
    row_count = moe_input.shape[0]
    quarter = moe_input.shape[1] // GROUP
    hidden_width = expert_gate.shape[1]
    out_cols = expert_down.shape[1]
    matches = expert_ids[:, :, None] == jnp.arange(hosted, dtype=jnp.int32)[None, None, :]
    routed = jnp.any(matches, axis=1).astype(jnp.int32)
    route_gain = jnp.sum(jnp.where(matches, route_weights[:, :, None], 0.0), axis=1)
    slot_rank = jnp.cumsum(routed, axis=0) - routed
    selector = (slot_rank.T[:, None, :] == jnp.arange(CAP, dtype=jnp.int32)[None, :, None]) & (
        routed.T[:, None, :] > 0
    )
    quarters = moe_input.reshape(row_count, GROUP, quarter)
    outgoing = jnp.einsum(
        "ecr,rqd->eqcd", selector.astype(jnp.bfloat16), quarters, preferred_element_type=jnp.float32
    )
    outgoing = outgoing.astype(jnp.bfloat16).reshape(hosted * GROUP, CAP, quarter)
    arrived = lax.all_to_all(outgoing, "wide", split_axis=0, concat_axis=1, tiled=True).reshape(
        wide_count * CAP, quarter
    )
    segment = lax.all_gather(arrived, "narrow", axis=0, tiled=True)
    gate_part = jnp.dot(segment, expert_gate, preferred_element_type=jnp.float32)
    up_part = jnp.dot(segment, expert_up, preferred_element_type=jnp.float32)
    partial_sums = jnp.concatenate([gate_part, up_part], axis=1)
    summed = partial_sums
    for level in range(2):
        summed = summed + from_partner(summed, "wide", level)
    hidden = (jax.nn.silu(summed[:, :hidden_width]) * summed[:, hidden_width:]).astype(jnp.bfloat16)
    expert_out = jnp.dot(
        lax.all_gather(hidden, "narrow", axis=1, tiled=True),
        expert_down,
        preferred_element_type=jnp.float32,
    ).astype(jnp.bfloat16)
    sectioned = expert_out.reshape(narrow_count, wide_count, CAP, 1, out_cols)
    returned = lax.all_to_all(
        lax.all_to_all(sectioned, "wide", split_axis=1, concat_axis=3, tiled=True),
        "narrow",
        split_axis=0,
        concat_axis=4,
        tiled=True,
    )
    returned = returned.reshape(CAP, hosted, GROUP * quarter)
    weighted = selector.astype(jnp.float32) * route_gain.T[:, None, :]
    combined = jnp.einsum(
        "ecr,ced->rd", weighted, returned.astype(jnp.float32), precision=lax.Precision.HIGHEST
    )
    return combined.astype(jnp.bfloat16)


def solution(mesh):
    in_specs = (
        P(("grp", "wide", "narrow"), None),
        P(("grp", "wide", "narrow"), None),
        P(("grp", "wide", "narrow"), None),
        P("wide", "narrow"),
        P("wide", "narrow"),
        P(None, ("wide", "narrow")),
    )
    out_specs = P(("grp", "wide", "narrow"), None)
    single = mesh.shape["wide"] == GROUP and mesh.shape["narrow"] == 4
    per_device = grouped if single else shards
    return jax.shard_map(per_device, mesh=mesh, in_specs=in_specs, out_specs=out_specs, check_vma=False)
```

```python
import functools

import jax
import jax.numpy as jnp
from jax import lax
from jax.experimental import pallas as pl
from jax.experimental.pallas import tpu as pltpu
from jax.sharding import PartitionSpec as P

GROUP = 4
CAP = 8
MESH = pl.DeviceIdType.MESH
F32 = jnp.float32
BF16 = jnp.bfloat16


def slot_rows(ids):
    rows = ids.shape[1]
    routed = jnp.sum(jnp.where(ids == 0, 1.0, 0.0), axis=0, keepdims=True)
    routed = jnp.broadcast_to(routed, (16, rows))
    before = lax.broadcasted_iota(jnp.int32, (rows, rows), 0) < lax.broadcasted_iota(jnp.int32, (rows, rows), 1)
    rank = jnp.dot(routed.astype(BF16), before.astype(F32).astype(BF16), preferred_element_type=F32)
    slot = lax.broadcasted_iota(jnp.int32, (16, rows), 0)
    slot = jnp.where(slot >= CAP, slot - CAP, slot).astype(F32)
    return jnp.where((rank == slot) & (routed > 0.5), 1.0, 0.0).astype(BF16)


def expert_kernel(
    ids_hbm, x_hbm, gate_hbm, up_hbm, down_hbm, ret_ref,
    x_v, gu_v, down_v, xq, seg, lhs, pbuf, rs, own, hid, obuf, ret, ids_v,
    ids_sem, x_sem, gu_sem, down_sem,
    a_send, a_recv, b_send, b_recv, c_send, c_recv,
    r_send, r_recv,
    ha_send, ha_recv, hb_send, hb_recv, hc_send, hc_recv,
    o_send, o_recv,
):
    w = lax.axis_index("wide")
    n = lax.axis_index("narrow")
    me = w * 4 + n
    mate = n + 1 - 2 * lax.rem(n, 2)
    across = lax.rem(n + 2, 4)
    diag = lax.rem(mate + 2, 4)
    quarter = gate_hbm.shape[0]
    half = quarter // 2
    block = gate_hbm.shape[1] // 4
    rows = lhs.shape[0]

    def ahead(k):
        return lax.rem(w + k, 4)

    def behind(k):
        return lax.rem(w + 4 - k, 4)

    barrier = pltpu.get_barrier_semaphore()
    for device in [{"wide": ahead(k)} for k in (2, 1, 3)] + [{"narrow": across}, {"narrow": mate}]:
        pl.semaphore_signal(barrier, inc=1, device_id=device, device_id_type=MESH)

    load_ids = pltpu.make_async_copy(ids_hbm, ids_v, ids_sem.at[0])
    load_ids.start()
    loads_x = []
    for k in (2, 1, 3, 0):
        cols = pl.ds(pl.multiple_of(ahead(k) * quarter, 128), quarter)
        loads_x.append(pltpu.make_async_copy(x_hbm.at[:, cols], x_v.at[k], x_sem.at[k]))
    for copy in loads_x:
        copy.start()
    loads_gu = []
    for j in range(4):
        for half_no, src in ((0, gate_hbm), (1, up_hbm)):
            loads_gu.append(
                pltpu.make_async_copy(
                    src.at[:, pl.ds(j * block, block)],
                    gu_v.at[:, pl.ds((2 * j + half_no) * block, block)],
                    gu_sem.at[2 * j + half_no],
                )
            )
    for copy in loads_gu:
        copy.start()
    load_down = pltpu.make_async_copy(down_hbm, down_v, down_sem.at[0])
    load_down.start()

    load_ids.wait()
    pick = slot_rows(ids_v[...])

    def gathered(k):
        first = jnp.dot(pick, x_v[k, :, :half], preferred_element_type=F32)
        second = jnp.dot(pick, x_v[k, :, half:], preferred_element_type=F32)
        return jnp.concatenate([first[:CAP], second[CAP:]], axis=0).astype(BF16)

    pl.semaphore_wait(barrier, 5)

    def remote(src, dst, send, recv, device):
        return pltpu.make_async_remote_copy(
            src_ref=src, dst_ref=dst, send_sem=send, recv_sem=recv, device_id=device, device_id_type=MESH
        )

    started = []

    def go(copy):
        copy.start()
        started.append(copy)
        return copy

    def spread(buf, place, a_copies, bs, br, cs, cr):
        cross = {}
        close = {}
        last = {}

        def forward(k):
            s = place(behind(k), n)
            close[k] = go(remote(buf.at[s], buf.at[s], bs.at[k], br.at[k], {"narrow": mate}))
            cross[k] = go(remote(buf.at[s], buf.at[s], bs.at[4 + k], br.at[4 + k], {"narrow": across}))

        def relay(k):
            cross[k].wait_recv()
            s = place(behind(k), across)
            last[k] = go(remote(buf.at[s], buf.at[s], cs.at[k], cr.at[k], {"narrow": mate}))

        forward(0)
        order = (0, 1, 3, 2)
        for i in range(1, 4):
            a_copies[order[i]].wait_recv()
            forward(order[i])
            relay(order[i - 1])
        relay(order[3])
        return close, last

    seg_place = lambda w_, n_: w_ * 4 + n_
    a_copies = {}
    for i, k in enumerate((2, 1, 3, 0)):
        loads_x[i].wait()
        value = gathered(k)
        if k:
            xq[k] = value
            a_copies[k] = go(
                remote(xq.at[k], seg.at[me], a_send.at[k], a_recv.at[k], {"wide": ahead(k)})
            )
        else:
            seg[me] = value
    close, last = spread(seg, seg_place, a_copies, b_send, b_recv, c_send, c_recv)
    for k in range(4):
        close[k].wait_recv()
    for k in range(4):
        last[k].wait_recv()
    for j in range(4):
        part = seg[4 * j:4 * j + 4].astype(F32)
        lhs[32 * j:32 * j + 32, :half] = part[:, :CAP].reshape(32, half).astype(BF16)
        lhs[32 * j:32 * j + 32, half:] = part[:, CAP:].reshape(32, half).astype(BF16)
    for copy in loads_gu:
        copy.wait()

    r_copies = {}
    for k in (2, 1, 3, 0):
        cols = pl.ds(pl.multiple_of(ahead(k) * 2 * block, 128), 2 * block)
        value = jnp.dot(lhs[...], gu_v[:, cols], preferred_element_type=F32)
        if k:
            pbuf[k] = value.astype(BF16)
            r_copies[k] = go(remote(pbuf.at[k], rs.at[k], r_send.at[k], r_recv.at[k], {"wide": ahead(k)}))
        else:
            own[...] = value
    for k in (1, 3, 2):
        r_copies[k].wait_recv()
    total = own[...] + rs[1].astype(F32) + rs[3].astype(F32) + rs[2].astype(F32)
    gate, up = total[:, :block], total[:, block:]
    mine = n * 4 + w
    hid[mine] = (gate / (1.0 + jnp.exp(-gate)) * up).astype(BF16)

    hid_place = lambda w_, n_: n_ * 4 + w_
    h_copies = {}
    for k in (2, 1, 3):
        h_copies[k] = go(
            remote(hid.at[mine], hid.at[mine], ha_send.at[k], ha_recv.at[k], {"wide": ahead(k)})
        )
    close, last = spread(hid, hid_place, h_copies, hb_send, hb_recv, hc_send, hc_recv)
    load_down.wait()

    def down_part(n_):
        left = jnp.concatenate([hid[n_ * 4 + j] for j in range(4)], axis=1)
        right = down_v[:, pl.ds(pl.multiple_of(n_ * 4 * block, 128), 4 * block)]
        return lax.dot_general(left, right, (((1,), (1,)), ((), ())), preferred_element_type=F32)

    out = down_part(n)
    out = out + down_part(across)
    for k in range(4):
        close[k].wait_recv()
    out = out + down_part(mate)
    for k in range(4):
        last[k].wait_recv()
    out = out + down_part(diag)

    width = out.shape[1]
    wide_half = obuf.shape[2]
    first = out[:, :wide_half].reshape(16, CAP, wide_half)
    second = jnp.concatenate(
        [out[:, wide_half:], jnp.zeros((rows, 2 * wide_half - width), F32)], axis=1
    ).reshape(16, CAP, wide_half)
    obuf[...] = jnp.concatenate([first, second], axis=1).astype(BF16)
    o_copies = []
    for t in range(1, 16):
        d = lax.rem(me + t, 16)
        o_copies.append(
            go(
                remote(
                    obuf.at[d], ret.at[me], o_send.at[t], o_recv.at[t],
                    {"wide": d // 4, "narrow": lax.rem(d, 4)},
                )
            )
        )
    ret[me] = obuf[me]
    for copy in o_copies:
        copy.wait_recv()
    ret_ref[...] = ret[...]
    for copy in started:
        copy.wait_send()


def combine_kernel(width, ids_ref, weights_ref, ret_ref, out_ref):
    ids = ids_ref[...]
    rows = ids.shape[1]
    hit = ids == 0
    gain = jnp.sum(jnp.where(hit, weights_ref[...], 0.0), axis=0, keepdims=True)
    gain = jnp.transpose(jnp.broadcast_to(gain, (128, rows)))
    place = slot_rows(ids)
    place = jnp.where(lax.broadcasted_iota(jnp.int32, place.shape, 0) < CAP, place.astype(F32), 0.0).astype(BF16)
    pieces = []
    wide_half = ret_ref.shape[2]
    for j in range(ret_ref.shape[0]):
        value = ret_ref[j].astype(F32)
        pieces += [value[:CAP], value[CAP:, :width - wide_half]]
    slots = jnp.concatenate(pieces, axis=1)
    slots = jnp.concatenate([slots, jnp.zeros_like(slots)], axis=0).astype(BF16)
    placed = lax.dot_general(place, slots, (((0,), (0,)), ((), ())), preferred_element_type=F32)
    gains = jnp.concatenate([gain] * (placed.shape[1] // 128), axis=1)
    out_ref[...] = (placed * gains).astype(BF16)


def grouped(moe_input, expert_ids, route_weights, expert_gate, expert_up, expert_down):
    rows, model = moe_input.shape
    quarter, hidden = expert_gate.shape
    width = expert_down.shape[1]
    block = hidden // 4
    wide_half = -(-width // 256) * 128
    all_rows = 16 * CAP
    ids, weights = expert_ids.T, route_weights.T
    dma = pltpu.SemaphoreType.DMA
    any_spec = pl.BlockSpec(memory_space=pl.ANY)
    vmem_spec = pl.BlockSpec(memory_space=pltpu.VMEM)
    returned = pl.pallas_call(
        expert_kernel,
        out_shape=jax.ShapeDtypeStruct((16, 16, wide_half), BF16),
        in_specs=[any_spec] * 5,
        out_specs=vmem_spec,
        scratch_shapes=[
            pltpu.VMEM((4, rows, quarter), BF16),
            pltpu.VMEM((quarter, 2 * hidden), BF16),
            pltpu.VMEM(expert_down.shape[::-1], BF16),
            pltpu.VMEM((4, 16, quarter // 2), BF16),
            pltpu.VMEM((16, 16, quarter // 2), BF16),
            pltpu.VMEM((all_rows, quarter), BF16),
            pltpu.VMEM((4, all_rows, 2 * block), BF16),
            pltpu.VMEM((4, all_rows, 2 * block), BF16),
            pltpu.VMEM((all_rows, 2 * block), F32),
            pltpu.VMEM((16, all_rows, block), BF16),
            pltpu.VMEM((16, 16, wide_half), BF16),
            pltpu.VMEM((16, 16, wide_half), BF16),
            pltpu.VMEM(ids.shape, jnp.int32),
            dma((1,)), dma((4,)), dma((8,)), dma((1,)),
            dma((4,)), dma((4,)), dma((8,)), dma((8,)), dma((4,)), dma((4,)),
            dma((4,)), dma((4,)),
            dma((4,)), dma((4,)), dma((8,)), dma((8,)), dma((4,)), dma((4,)),
            dma((16,)), dma((16,)),
        ],
        compiler_params=pltpu.CompilerParams(
            collective_id=0, has_side_effects=True, vmem_limit_bytes=56 * 1024 * 1024
        ),
    )(ids, moe_input, expert_gate, expert_up, expert_down.T)
    parts = 1
    return pl.pallas_call(
        functools.partial(combine_kernel, width),
        out_shape=jax.ShapeDtypeStruct((rows, model), BF16),
        grid=(parts,),
        in_specs=[
            pl.BlockSpec(ids.shape, lambda i: (0, 0)),
            pl.BlockSpec(weights.shape, lambda i: (0, 0)),
            pl.BlockSpec((16 // parts, 16, wide_half), lambda i: (i, 0, 0)),
        ],
        out_specs=pl.BlockSpec((rows, model // parts), lambda i: (0, i)),
    )(ids, weights, returned)


def from_partner(block, axis, stride):
    count = lax.axis_size(axis)
    route = []
    for low in range(count):
        high = low | 1 << stride
        if high != low and high < count:
            route += [(low, high), (high, low)]
    return lax.ppermute(block, axis, route)


def shards(moe_input, expert_ids, route_weights, expert_gate, expert_up, expert_down):
    wide_count = lax.axis_size("wide")
    narrow_count = lax.axis_size("narrow")
    hosted = wide_count // GROUP
    row_count = moe_input.shape[0]
    quarter = moe_input.shape[1] // GROUP
    hidden_width = expert_gate.shape[1]
    out_cols = expert_down.shape[1]
    matches = expert_ids[:, :, None] == jnp.arange(hosted, dtype=jnp.int32)[None, None, :]
    routed = jnp.any(matches, axis=1).astype(jnp.int32)
    route_gain = jnp.sum(jnp.where(matches, route_weights[:, :, None], 0.0), axis=1)
    slot_rank = jnp.cumsum(routed, axis=0) - routed
    selector = (slot_rank.T[:, None, :] == jnp.arange(CAP, dtype=jnp.int32)[None, :, None]) & (
        routed.T[:, None, :] > 0
    )
    quarters = moe_input.reshape(row_count, GROUP, quarter)
    outgoing = jnp.einsum(
        "ecr,rqd->eqcd", selector.astype(jnp.bfloat16), quarters, preferred_element_type=jnp.float32
    )
    outgoing = outgoing.astype(jnp.bfloat16).reshape(hosted * GROUP, CAP, quarter)
    arrived = lax.all_to_all(outgoing, "wide", split_axis=0, concat_axis=1, tiled=True).reshape(
        wide_count * CAP, quarter
    )
    segment = lax.all_gather(arrived, "narrow", axis=0, tiled=True)
    gate_part = jnp.dot(segment, expert_gate, preferred_element_type=jnp.float32)
    up_part = jnp.dot(segment, expert_up, preferred_element_type=jnp.float32)
    partial_sums = jnp.concatenate([gate_part, up_part], axis=1)
    summed = partial_sums
    for level in range(2):
        summed = summed + from_partner(summed, "wide", level)
    hidden = (jax.nn.silu(summed[:, :hidden_width]) * summed[:, hidden_width:]).astype(jnp.bfloat16)
    expert_out = jnp.dot(
        lax.all_gather(hidden, "narrow", axis=1, tiled=True),
        expert_down,
        preferred_element_type=jnp.float32,
    ).astype(jnp.bfloat16)
    sectioned = expert_out.reshape(narrow_count, wide_count, CAP, 1, out_cols)
    returned = lax.all_to_all(
        lax.all_to_all(sectioned, "wide", split_axis=1, concat_axis=3, tiled=True),
        "narrow",
        split_axis=0,
        concat_axis=4,
        tiled=True,
    )
    returned = returned.reshape(CAP, hosted, GROUP * quarter)
    weighted = selector.astype(jnp.float32) * route_gain.T[:, None, :]
    combined = jnp.einsum(
        "ecr,ced->rd", weighted, returned.astype(jnp.float32), precision=lax.Precision.HIGHEST
    )
    return combined.astype(jnp.bfloat16)


def solution(mesh):
    in_specs = (
        P(("grp", "wide", "narrow"), None),
        P(("grp", "wide", "narrow"), None),
        P(("grp", "wide", "narrow"), None),
        P("wide", "narrow"),
        P("wide", "narrow"),
        P(None, ("wide", "narrow")),
    )
    out_specs = P(("grp", "wide", "narrow"), None)
    single = mesh.shape["wide"] == GROUP and mesh.shape["narrow"] == 4
    per_device = grouped if single else shards
    return jax.shard_map(per_device, mesh=mesh, in_specs=in_specs, out_specs=out_specs, check_vma=False)
```

```python
import functools

import jax
import jax.numpy as jnp
from jax import lax
from jax.experimental import pallas as pl
from jax.experimental.pallas import tpu as pltpu
from jax.sharding import PartitionSpec as P

GROUP = 4
CAP = 8
MESH = pl.DeviceIdType.MESH
F32 = jnp.float32
BF16 = jnp.bfloat16


def slot_rows(ids):
    rows = ids.shape[1]
    routed = jnp.sum(jnp.where(ids == 0, 1.0, 0.0), axis=0, keepdims=True)
    routed = jnp.broadcast_to(routed, (16, rows))
    before = lax.broadcasted_iota(jnp.int32, (rows, rows), 0) < lax.broadcasted_iota(jnp.int32, (rows, rows), 1)
    rank = jnp.dot(routed.astype(BF16), before.astype(F32).astype(BF16), preferred_element_type=F32)
    slot = lax.broadcasted_iota(jnp.int32, (16, rows), 0)
    slot = jnp.where(slot >= CAP, slot - CAP, slot).astype(F32)
    return jnp.where((rank == slot) & (routed > 0.5), 1.0, 0.0).astype(BF16)


def expert_kernel(
    ids_hbm, x_hbm, gate_hbm, up_hbm, down_hbm, ret_ref,
    x_v, gu_v, down_v, xq, seg, lhs, pbuf, rs, own, hid, obuf, ret, ids_v,
    ids_sem, x_sem, gu_sem, down_sem,
    a_send, a_recv, b_send, b_recv, c_send, c_recv,
    r_send, r_recv,
    ha_send, ha_recv, hb_send, hb_recv, hc_send, hc_recv,
    o_send, o_recv,
):
    w = lax.axis_index("wide")
    n = lax.axis_index("narrow")
    me = w * 4 + n
    mate = n + 1 - 2 * lax.rem(n, 2)
    across = lax.rem(n + 2, 4)
    diag = lax.rem(mate + 2, 4)
    quarter = gate_hbm.shape[0]
    half = quarter // 2
    block = gate_hbm.shape[1] // 4
    rows = 2 * lhs.shape[1]

    def ahead(k):
        return lax.rem(w + k, 4)

    def behind(k):
        return lax.rem(w + 4 - k, 4)

    barrier = pltpu.get_barrier_semaphore()
    for device in [{"wide": ahead(k)} for k in (2, 1, 3)] + [{"narrow": across}, {"narrow": mate}]:
        pl.semaphore_signal(barrier, inc=1, device_id=device, device_id_type=MESH)

    load_ids = pltpu.make_async_copy(ids_hbm, ids_v, ids_sem.at[0])
    load_ids.start()
    loads_x = []
    for k in (2, 1, 3, 0):
        cols = pl.ds(pl.multiple_of(ahead(k) * quarter, 128), quarter)
        loads_x.append(pltpu.make_async_copy(x_hbm.at[:, cols], x_v.at[k], x_sem.at[k]))
    for copy in loads_x:
        copy.start()
    loads_gu = []
    for j in range(4):
        for half_no, src in ((0, gate_hbm), (1, up_hbm)):
            loads_gu.append(
                pltpu.make_async_copy(
                    src.at[:, pl.ds(j * block, block)],
                    gu_v.at[:, pl.ds((2 * j + half_no) * block, block)],
                    gu_sem.at[2 * j + half_no],
                )
            )
    for copy in loads_gu:
        copy.start()
    load_down = pltpu.make_async_copy(down_hbm, down_v, down_sem.at[0])
    load_down.start()

    load_ids.wait()
    pick = slot_rows(ids_v[...])

    def gathered(k):
        first = jnp.dot(pick, x_v[k, :, :half], preferred_element_type=F32)
        second = jnp.dot(pick, x_v[k, :, half:], preferred_element_type=F32)
        return jnp.concatenate([first[:CAP], second[CAP:]], axis=0).astype(BF16)

    pl.semaphore_wait(barrier, 5)

    def remote(src, dst, send, recv, device):
        return pltpu.make_async_remote_copy(
            src_ref=src, dst_ref=dst, send_sem=send, recv_sem=recv, device_id=device, device_id_type=MESH
        )

    started = []

    def go(copy):
        copy.start()
        started.append(copy)
        return copy

    class Spread:
        def __init__(self, buf, place, bs, br, cs, cr, base):
            self.buf, self.place, self.base = buf, place, base
            self.sems = bs, br, cs, cr
            self.cross, self.close, self.last = {}, {}, {}

        def forward(self, k):
            bs, br, _, _ = self.sems
            block_ref = self.buf.at[self.place(behind(k), n)]
            i = self.base + k
            self.cross[k] = go(remote(block_ref, block_ref, bs.at[2 * i], br.at[2 * i], {"narrow": across}))
            self.close[k] = go(remote(block_ref, block_ref, bs.at[2 * i + 1], br.at[2 * i + 1], {"narrow": mate}))

        def relay(self, k):
            _, _, cs, cr = self.sems
            self.cross[k].wait_recv()
            block_ref = self.buf.at[self.place(behind(k), across)]
            i = self.base + k
            self.last[k] = go(remote(block_ref, block_ref, cs.at[i], cr.at[i], {"narrow": mate}))

        def wait_close(self):
            for k in self.close:
                self.close[k].wait_recv()

        def wait_last(self):
            for k in self.last:
                self.last[k].wait_recv()

    def seg_place(w_, n_):
        return (n_ // 2) * 8 + w_ * 2 + lax.rem(n_, 2)

    seg_mine = seg_place(w, n)
    a_copies = {}
    for i, k in enumerate((2, 1, 3, 0)):
        loads_x[i].wait()
        value = gathered(k)
        if k:
            xq[k] = value
            a_copies[k] = go(
                remote(xq.at[k], seg.at[seg_mine], a_send.at[k], a_recv.at[k], {"wide": ahead(k)})
            )
        else:
            seg[seg_mine] = value
    spread = Spread(seg, seg_place, b_send, b_recv, c_send, c_recv, 0)
    spread.forward(0)
    a_copies[1].wait_recv()
    spread.forward(1)
    spread.relay(0)
    a_copies[3].wait_recv()
    spread.forward(3)
    spread.relay(1)
    a_copies[2].wait_recv()
    spread.forward(2)
    spread.relay(3)
    spread.wait_close()

    side = n // 2
    part_rows = rows // 2

    def fill(c):
        part_side = side if c == 0 else 1 - side
        part = seg[pl.ds(part_side * 8, 8)].astype(F32)
        lhs[c, :, :half] = part[:, :CAP].reshape(part_rows, half).astype(BF16)
        lhs[c, :, half:] = part[:, CAP:].reshape(part_rows, half).astype(BF16)

    r_copies = {}

    def partial_sums(c, k):
        cols = pl.ds(pl.multiple_of(ahead(k) * 2 * block, 128), 2 * block)
        value = jnp.dot(lhs[c], gu_v[:, cols], preferred_element_type=F32)
        if k:
            i = 4 * c + k
            pbuf[i] = value.astype(BF16)
            r_copies[i] = go(remote(pbuf.at[i], rs.at[i], r_send.at[i], r_recv.at[i], {"wide": ahead(k)}))
        else:
            own[c] = value

    fill(0)
    for copy in loads_gu:
        copy.wait()
    partial_sums(0, 2)
    partial_sums(0, 1)
    partial_sums(0, 3)
    spread.relay(2)
    partial_sums(0, 0)
    spread.wait_last()
    fill(1)
    for k in (2, 1, 3, 0):
        partial_sums(1, k)

    h_copies = {}
    h_spread = {}

    def hid_place(c):
        def place(w_, n_):
            n_side = n_ // 2
            return (n_side if c == 0 else 1 - n_side) * 16 + n_ * 4 + w_

        return place

    for c in range(2):
        for k in (1, 3, 2):
            r_copies[4 * c + k].wait_recv()
        total = own[c]
        for k in (1, 3, 2):
            total = total + rs[4 * c + k].astype(F32)
        gate, up = total[:, :block], total[:, block:]
        place = hid_place(c)
        mine = place(w, n)
        hid[mine] = (gate / (1.0 + jnp.exp(-gate)) * up).astype(BF16)
        for k in (2, 1, 3):
            i = 4 * c + k
            h_copies[i] = go(
                remote(hid.at[mine], hid.at[mine], ha_send.at[i], ha_recv.at[i], {"wide": ahead(k)})
            )
        h_spread[c] = Spread(hid, place, hb_send, hb_recv, hc_send, hc_recv, 4 * c)
        h_spread[c].forward(0)
    late = []
    for c in range(2):
        for done, k in ((0, 1), (1, 3), (3, 2)):
            h_copies[4 * c + k].wait_recv()
            h_spread[c].forward(k)
            late.append((c, done))
            if len(late) > 1:
                before_c, before_k = late.pop(0)
                h_spread[before_c].relay(before_k)
        late.append((c, 2))
    for before_c, before_k in late:
        h_spread[before_c].relay(before_k)
    load_down.wait()

    def down_part(n_):
        left = jnp.concatenate(
            [
                jnp.concatenate([hid[16 * s + n_ * 4 + j] for j in range(4)], axis=1)
                for s in range(2)
            ],
            axis=0,
        )
        right = down_v[:, pl.ds(pl.multiple_of(n_ * 4 * block, 128), 4 * block)]
        return lax.dot_general(left, right, (((1,), (1,)), ((), ())), preferred_element_type=F32)

    out = down_part(n)
    out = out + down_part(across)
    for c in range(2):
        h_spread[c].wait_close()
    out = out + down_part(mate)
    for c in range(2):
        h_spread[c].wait_last()
    out = out + down_part(diag)

    width = out.shape[1]
    wide_half = obuf.shape[2]
    first = out[:, :wide_half].reshape(16, CAP, wide_half)
    second = jnp.concatenate(
        [out[:, wide_half:], jnp.zeros((rows, 2 * wide_half - width), F32)], axis=1
    ).reshape(16, CAP, wide_half)
    obuf[...] = jnp.concatenate([first, second], axis=1).astype(BF16)
    o_copies = []
    for t in range(1, 16):
        d = lax.rem(me + t, 16)
        o_copies.append(
            go(
                remote(
                    obuf.at[seg_place(d // 4, lax.rem(d, 4))], ret.at[me], o_send.at[t], o_recv.at[t],
                    {"wide": d // 4, "narrow": lax.rem(d, 4)},
                )
            )
        )
    ret[me] = obuf[seg_mine]
    for copy in o_copies:
        copy.wait_recv()
    ret_ref[...] = ret[...]
    for copy in started:
        copy.wait_send()


def combine_kernel(width, ids_ref, weights_ref, ret_ref, out_ref):
    ids = ids_ref[...]
    rows = ids.shape[1]
    hit = ids == 0
    gain = jnp.sum(jnp.where(hit, weights_ref[...], 0.0), axis=0, keepdims=True)
    gain = jnp.transpose(jnp.broadcast_to(gain, (128, rows)))
    place = slot_rows(ids)
    place = jnp.where(lax.broadcasted_iota(jnp.int32, place.shape, 0) < CAP, place.astype(F32), 0.0).astype(BF16)
    pieces = []
    wide_half = ret_ref.shape[2]
    for j in range(ret_ref.shape[0]):
        value = ret_ref[j].astype(F32)
        pieces += [value[:CAP], value[CAP:, :width - wide_half]]
    slots = jnp.concatenate(pieces, axis=1)
    slots = jnp.concatenate([slots, jnp.zeros_like(slots)], axis=0).astype(BF16)
    placed = lax.dot_general(place, slots, (((0,), (0,)), ((), ())), preferred_element_type=F32)
    gains = jnp.concatenate([gain] * (placed.shape[1] // 128), axis=1)
    out_ref[...] = (placed * gains).astype(BF16)


def grouped(moe_input, expert_ids, route_weights, expert_gate, expert_up, expert_down):
    rows, model = moe_input.shape
    quarter, hidden = expert_gate.shape
    width = expert_down.shape[1]
    block = hidden // 4
    wide_half = -(-width // 256) * 128
    part_rows = 8 * CAP
    ids, weights = expert_ids.T, route_weights.T
    dma = pltpu.SemaphoreType.DMA
    any_spec = pl.BlockSpec(memory_space=pl.ANY)
    vmem_spec = pl.BlockSpec(memory_space=pltpu.VMEM)
    returned = pl.pallas_call(
        expert_kernel,
        out_shape=jax.ShapeDtypeStruct((16, 16, wide_half), BF16),
        in_specs=[any_spec] * 5,
        out_specs=vmem_spec,
        scratch_shapes=[
            pltpu.VMEM((4, rows, quarter), BF16),
            pltpu.VMEM((quarter, 2 * hidden), BF16),
            pltpu.VMEM(expert_down.shape[::-1], BF16),
            pltpu.VMEM((4, 16, quarter // 2), BF16),
            pltpu.VMEM((16, 16, quarter // 2), BF16),
            pltpu.VMEM((2, part_rows, quarter), BF16),
            pltpu.VMEM((8, part_rows, 2 * block), BF16),
            pltpu.VMEM((8, part_rows, 2 * block), BF16),
            pltpu.VMEM((2, part_rows, 2 * block), F32),
            pltpu.VMEM((32, part_rows, block), BF16),
            pltpu.VMEM((16, 16, wide_half), BF16),
            pltpu.VMEM((16, 16, wide_half), BF16),
            pltpu.VMEM(ids.shape, jnp.int32),
            dma((1,)), dma((4,)), dma((8,)), dma((1,)),
            dma((4,)), dma((4,)), dma((8,)), dma((8,)), dma((4,)), dma((4,)),
            dma((8,)), dma((8,)),
            dma((8,)), dma((8,)), dma((16,)), dma((16,)), dma((8,)), dma((8,)),
            dma((16,)), dma((16,)),
        ],
        compiler_params=pltpu.CompilerParams(
            collective_id=0, has_side_effects=True, vmem_limit_bytes=56 * 1024 * 1024
        ),
    )(ids, moe_input, expert_gate, expert_up, expert_down.T)
    parts = 1
    return pl.pallas_call(
        functools.partial(combine_kernel, width),
        out_shape=jax.ShapeDtypeStruct((rows, model), BF16),
        grid=(parts,),
        in_specs=[
            pl.BlockSpec(ids.shape, lambda i: (0, 0)),
            pl.BlockSpec(weights.shape, lambda i: (0, 0)),
            pl.BlockSpec((16 // parts, 16, wide_half), lambda i: (i, 0, 0)),
        ],
        out_specs=pl.BlockSpec((rows, model // parts), lambda i: (0, i)),
    )(ids, weights, returned)


def from_partner(block, axis, stride):
    count = lax.axis_size(axis)
    route = []
    for low in range(count):
        high = low | 1 << stride
        if high != low and high < count:
            route += [(low, high), (high, low)]
    return lax.ppermute(block, axis, route)


def shards(moe_input, expert_ids, route_weights, expert_gate, expert_up, expert_down):
    wide_count = lax.axis_size("wide")
    narrow_count = lax.axis_size("narrow")
    hosted = wide_count // GROUP
    row_count = moe_input.shape[0]
    quarter = moe_input.shape[1] // GROUP
    hidden_width = expert_gate.shape[1]
    out_cols = expert_down.shape[1]
    matches = expert_ids[:, :, None] == jnp.arange(hosted, dtype=jnp.int32)[None, None, :]
    routed = jnp.any(matches, axis=1).astype(jnp.int32)
    route_gain = jnp.sum(jnp.where(matches, route_weights[:, :, None], 0.0), axis=1)
    slot_rank = jnp.cumsum(routed, axis=0) - routed
    selector = (slot_rank.T[:, None, :] == jnp.arange(CAP, dtype=jnp.int32)[None, :, None]) & (
        routed.T[:, None, :] > 0
    )
    quarters = moe_input.reshape(row_count, GROUP, quarter)
    outgoing = jnp.einsum(
        "ecr,rqd->eqcd", selector.astype(jnp.bfloat16), quarters, preferred_element_type=jnp.float32
    )
    outgoing = outgoing.astype(jnp.bfloat16).reshape(hosted * GROUP, CAP, quarter)
    arrived = lax.all_to_all(outgoing, "wide", split_axis=0, concat_axis=1, tiled=True).reshape(
        wide_count * CAP, quarter
    )
    segment = lax.all_gather(arrived, "narrow", axis=0, tiled=True)
    gate_part = jnp.dot(segment, expert_gate, preferred_element_type=jnp.float32)
    up_part = jnp.dot(segment, expert_up, preferred_element_type=jnp.float32)
    partial_sums = jnp.concatenate([gate_part, up_part], axis=1)
    summed = partial_sums
    for level in range(2):
        summed = summed + from_partner(summed, "wide", level)
    hidden = (jax.nn.silu(summed[:, :hidden_width]) * summed[:, hidden_width:]).astype(jnp.bfloat16)
    expert_out = jnp.dot(
        lax.all_gather(hidden, "narrow", axis=1, tiled=True),
        expert_down,
        preferred_element_type=jnp.float32,
    ).astype(jnp.bfloat16)
    sectioned = expert_out.reshape(narrow_count, wide_count, CAP, 1, out_cols)
    returned = lax.all_to_all(
        lax.all_to_all(sectioned, "wide", split_axis=1, concat_axis=3, tiled=True),
        "narrow",
        split_axis=0,
        concat_axis=4,
        tiled=True,
    )
    returned = returned.reshape(CAP, hosted, GROUP * quarter)
    weighted = selector.astype(jnp.float32) * route_gain.T[:, None, :]
    combined = jnp.einsum(
        "ecr,ced->rd", weighted, returned.astype(jnp.float32), precision=lax.Precision.HIGHEST
    )
    return combined.astype(jnp.bfloat16)


def solution(mesh):
    in_specs = (
        P(("grp", "wide", "narrow"), None),
        P(("grp", "wide", "narrow"), None),
        P(("grp", "wide", "narrow"), None),
        P("wide", "narrow"),
        P("wide", "narrow"),
        P(None, ("wide", "narrow")),
    )
    out_specs = P(("grp", "wide", "narrow"), None)
    single = mesh.shape["wide"] == GROUP and mesh.shape["narrow"] == 4
    per_device = grouped if single else shards
    return jax.shard_map(per_device, mesh=mesh, in_specs=in_specs, out_specs=out_specs, check_vma=False)
```

```python
import functools

import jax
import jax.numpy as jnp
from jax import lax
from jax.experimental import pallas as pl
from jax.experimental.pallas import tpu as pltpu
from jax.sharding import PartitionSpec as P

GROUP = 4
CAP = 8
MESH = pl.DeviceIdType.MESH
F32 = jnp.float32
BF16 = jnp.bfloat16
BOTH_ROWS = False
BOTH_HIDDEN = True


def slot_rows(ids):
    rows = ids.shape[1]
    routed = jnp.sum(jnp.where(ids == 0, 1.0, 0.0), axis=0, keepdims=True)
    routed = jnp.broadcast_to(routed, (16, rows))
    before = lax.broadcasted_iota(jnp.int32, (rows, rows), 0) < lax.broadcasted_iota(jnp.int32, (rows, rows), 1)
    rank = jnp.dot(routed.astype(BF16), before.astype(F32).astype(BF16), preferred_element_type=F32)
    slot = lax.broadcasted_iota(jnp.int32, (16, rows), 0)
    slot = jnp.where(slot >= CAP, slot - CAP, slot).astype(F32)
    return jnp.where((rank == slot) & (routed > 0.5), 1.0, 0.0).astype(BF16)


def expert_kernel(
    ids_hbm, x_hbm, gate_hbm, up_hbm, down_hbm, ret_ref,
    x_v, gu_v, down_v, xq, seg, lhs, pbuf, rs, own, hid, obuf, ret, ids_v,
    ids_sem, x_sem, gu_sem, down_sem,
    a_send, a_recv, b_send, b_recv, c_send, c_recv,
    r_send, r_recv,
    ha_send, ha_recv, hb_send, hb_recv, hc_send, hc_recv,
    o_send, o_recv,
):
    w = lax.axis_index("wide")
    n = lax.axis_index("narrow")
    me = w * 4 + n
    mate = n + 1 - 2 * lax.rem(n, 2)
    across = lax.rem(n + 2, 4)
    diag = lax.rem(mate + 2, 4)
    quarter = gate_hbm.shape[0]
    half = quarter // 2
    block = gate_hbm.shape[1] // 4
    rows = 2 * lhs.shape[1]

    def ahead(k):
        return lax.rem(w + k, 4)

    def behind(k):
        return lax.rem(w + 4 - k, 4)

    barrier = pltpu.get_barrier_semaphore()
    for device in [{"wide": ahead(k)} for k in (2, 1, 3)] + [{"narrow": m} for m in (across, diag, mate)]:
        pl.semaphore_signal(barrier, inc=1, device_id=device, device_id_type=MESH)

    load_ids = pltpu.make_async_copy(ids_hbm, ids_v, ids_sem.at[0])
    load_ids.start()
    loads_x = []
    for k in (2, 1, 3, 0):
        cols = pl.ds(pl.multiple_of(ahead(k) * quarter, 128), quarter)
        loads_x.append(pltpu.make_async_copy(x_hbm.at[:, cols], x_v.at[k], x_sem.at[k]))
    for copy in loads_x:
        copy.start()
    loads_gu = []
    for j in range(4):
        for half_no, src in ((0, gate_hbm), (1, up_hbm)):
            loads_gu.append(
                pltpu.make_async_copy(
                    src.at[:, pl.ds(j * block, block)],
                    gu_v.at[:, pl.ds((2 * j + half_no) * block, block)],
                    gu_sem.at[2 * j + half_no],
                )
            )
    for copy in loads_gu:
        copy.start()
    load_down = pltpu.make_async_copy(down_hbm, down_v, down_sem.at[0])
    load_down.start()

    load_ids.wait()
    pick = slot_rows(ids_v[...])

    def gathered(k):
        first = jnp.dot(pick, x_v[k, :, :half], preferred_element_type=F32)
        second = jnp.dot(pick, x_v[k, :, half:], preferred_element_type=F32)
        return jnp.concatenate([first[:CAP], second[CAP:]], axis=0).astype(BF16)

    pl.semaphore_wait(barrier, 6)

    def remote(src, dst, send, recv, device):
        return pltpu.make_async_remote_copy(
            src_ref=src, dst_ref=dst, send_sem=send, recv_sem=recv, device_id=device, device_id_type=MESH
        )

    started = []

    def go(copy):
        copy.start()
        started.append(copy)
        return copy

    class Spread:
        def __init__(self, buf, place, sems, base, both):
            self.buf, self.place, self.base, self.both = buf, place, base, both
            self.a_s, self.a_r, self.b_s, self.b_r, self.c_s, self.c_r = sems
            self.mine = buf.at[place(w, n)]
            self.near, self.cross, self.close, self.far = {}, {}, {}, {}

        def send_near(self, k, source):
            i = 2 * (self.base + k)
            self.near[k] = go(remote(source, self.mine, self.a_s.at[i], self.a_r.at[i], {"wide": ahead(k)}))

        def send_cross(self, k, source):
            if self.both:
                i = 2 * (self.base + k) + 1
                device = {"wide": ahead(k), "narrow": across}
                self.cross[k] = go(remote(source, self.mine, self.a_s.at[i], self.a_r.at[i], device))

        def forward(self, k):
            if k:
                self.near[k].wait_recv()
            i = self.base + k
            ref = self.buf.at[self.place(behind(k), n)]
            if not self.both:
                self.cross[k] = go(remote(ref, ref, self.b_s.at[2 * i], self.b_r.at[2 * i], {"narrow": across}))
                self.far[k] = go(remote(ref, ref, self.c_s.at[i], self.c_r.at[i], {"narrow": diag}))
            self.close[k] = go(remote(ref, ref, self.b_s.at[2 * i + 1], self.b_r.at[2 * i + 1], {"narrow": mate}))

        def forward_cross(self, k):
            if self.both:
                self.cross[k].wait_recv()
                i = self.base + k
                ref = self.buf.at[self.place(behind(k), across)]
                self.far[k] = go(remote(ref, ref, self.c_s.at[i], self.c_r.at[i], {"narrow": mate}))

        def wait_close(self):
            for k in self.close:
                self.close[k].wait_recv()

        def wait_cross(self):
            if not self.both:
                for k in self.cross:
                    self.cross[k].wait_recv()

        def wait_far(self):
            for k in self.far:
                self.far[k].wait_recv()

    def seg_place(w_, n_):
        return (n_ // 2) * 8 + w_ * 2 + lax.rem(n_, 2)

    seg_mine = seg_place(w, n)
    spread = Spread(seg, seg_place, (a_send, a_recv, b_send, b_recv, c_send, c_recv), 0, BOTH_ROWS)
    for i, k in enumerate((2, 1, 3, 0)):
        loads_x[i].wait()
        value = gathered(k)
        if k:
            xq[k] = value
            spread.send_near(k, xq.at[k])
        else:
            seg[seg_mine] = value
    for k in (2, 1, 3):
        spread.send_cross(k, xq.at[k])
    spread.send_cross(0, seg.at[seg_mine])
    for k in (0, 1, 3, 2):
        spread.forward(k)
    spread.wait_close()

    side = n // 2
    part_rows = rows // 2

    def fill(c):
        part_side = side if c == 0 else 1 - side
        part = seg[pl.ds(part_side * 8, 8)].astype(F32)
        lhs[c, :, :half] = part[:, :CAP].reshape(part_rows, half).astype(BF16)
        lhs[c, :, half:] = part[:, CAP:].reshape(part_rows, half).astype(BF16)

    r_copies = {}

    def partial_sums(c, k):
        cols = pl.ds(pl.multiple_of(ahead(k) * 2 * block, 128), 2 * block)
        value = jnp.dot(lhs[c], gu_v[:, cols], preferred_element_type=F32)
        if k:
            i = 4 * c + k
            pbuf[i] = value.astype(BF16)
            r_copies[i] = go(remote(pbuf.at[i], rs.at[i], r_send.at[i], r_recv.at[i], {"wide": ahead(k)}))
        else:
            own[c] = value

    fill(0)
    for copy in loads_gu:
        copy.wait()
    partial_sums(0, 2)
    partial_sums(0, 1)
    partial_sums(0, 3)
    partial_sums(0, 0)
    for k in (0, 1, 3, 2):
        spread.forward_cross(k)
    spread.wait_cross()
    spread.wait_far()
    fill(1)
    for k in (2, 1, 3, 0):
        partial_sums(1, k)

    h_spread = {}

    def hid_place(c):
        def place(w_, n_):
            n_side = n_ // 2
            return (n_side if c == 0 else 1 - n_side) * 16 + n_ * 4 + w_

        return place

    for c in range(2):
        for k in (1, 3, 2):
            r_copies[4 * c + k].wait_recv()
        total = own[c]
        for k in (1, 3, 2):
            total = total + rs[4 * c + k].astype(F32)
        gate, up = total[:, :block], total[:, block:]
        place = hid_place(c)
        mine = place(w, n)
        hid[mine] = (gate / (1.0 + jnp.exp(-gate)) * up).astype(BF16)
        h_spread[c] = Spread(
            hid, place, (ha_send, ha_recv, hb_send, hb_recv, hc_send, hc_recv), 4 * c, BOTH_HIDDEN
        )
        for k in (2, 1, 3):
            h_spread[c].send_near(k, hid.at[mine])
        for k in (2, 1, 3, 0):
            h_spread[c].send_cross(k, hid.at[mine])
        h_spread[c].forward(0)
    for c in range(2):
        for k in (1, 3, 2):
            h_spread[c].forward(k)
        for k in (0, 1, 3, 2):
            h_spread[c].forward_cross(k)
    load_down.wait()

    def down_part(n_):
        left = jnp.concatenate(
            [
                jnp.concatenate([hid[16 * s + n_ * 4 + j] for j in range(4)], axis=1)
                for s in range(2)
            ],
            axis=0,
        )
        right = down_v[:, pl.ds(pl.multiple_of(n_ * 4 * block, 128), 4 * block)]
        return lax.dot_general(left, right, (((1,), (1,)), ((), ())), preferred_element_type=F32)

    out = down_part(n)
    for c in range(2):
        h_spread[c].wait_close()
    out = out + down_part(mate)
    for c in range(2):
        h_spread[c].wait_cross()
    out = out + down_part(across)
    for c in range(2):
        h_spread[c].wait_far()
    out = out + down_part(diag)

    width = out.shape[1]
    wide_half = obuf.shape[2]
    first = out[:, :wide_half].reshape(16, CAP, wide_half)
    second = jnp.concatenate(
        [out[:, wide_half:], jnp.zeros((rows, 2 * wide_half - width), F32)], axis=1
    ).reshape(16, CAP, wide_half)
    obuf[...] = jnp.concatenate([first, second], axis=1).astype(BF16)
    o_copies = []
    for t in range(1, 16):
        d = lax.rem(me + t, 16)
        o_copies.append(
            go(
                remote(
                    obuf.at[seg_place(d // 4, lax.rem(d, 4))], ret.at[me], o_send.at[t], o_recv.at[t],
                    {"wide": d // 4, "narrow": lax.rem(d, 4)},
                )
            )
        )
    ret[me] = obuf[seg_mine]
    for copy in o_copies:
        copy.wait_recv()
    ret_ref[...] = ret[...]
    for copy in started:
        copy.wait_send()


def combine_kernel(width, ids_ref, weights_ref, ret_ref, out_ref):
    ids = ids_ref[...]
    rows = ids.shape[1]
    hit = ids == 0
    gain = jnp.sum(jnp.where(hit, weights_ref[...], 0.0), axis=0, keepdims=True)
    gain = jnp.transpose(jnp.broadcast_to(gain, (128, rows)))
    place = slot_rows(ids)
    place = jnp.where(lax.broadcasted_iota(jnp.int32, place.shape, 0) < CAP, place.astype(F32), 0.0).astype(BF16)
    pieces = []
    wide_half = ret_ref.shape[2]
    for j in range(ret_ref.shape[0]):
        value = ret_ref[j].astype(F32)
        pieces += [value[:CAP], value[CAP:, :width - wide_half]]
    slots = jnp.concatenate(pieces, axis=1)
    slots = jnp.concatenate([slots, jnp.zeros_like(slots)], axis=0).astype(BF16)
    placed = lax.dot_general(place, slots, (((0,), (0,)), ((), ())), preferred_element_type=F32)
    gains = jnp.concatenate([gain] * (placed.shape[1] // 128), axis=1)
    out_ref[...] = (placed * gains).astype(BF16)


def grouped(moe_input, expert_ids, route_weights, expert_gate, expert_up, expert_down):
    rows, model = moe_input.shape
    quarter, hidden = expert_gate.shape
    width = expert_down.shape[1]
    block = hidden // 4
    wide_half = -(-width // 256) * 128
    part_rows = 8 * CAP
    ids, weights = expert_ids.T, route_weights.T
    dma = pltpu.SemaphoreType.DMA
    any_spec = pl.BlockSpec(memory_space=pl.ANY)
    vmem_spec = pl.BlockSpec(memory_space=pltpu.VMEM)
    returned = pl.pallas_call(
        expert_kernel,
        out_shape=jax.ShapeDtypeStruct((16, 16, wide_half), BF16),
        in_specs=[any_spec] * 5,
        out_specs=vmem_spec,
        scratch_shapes=[
            pltpu.VMEM((4, rows, quarter), BF16),
            pltpu.VMEM((quarter, 2 * hidden), BF16),
            pltpu.VMEM(expert_down.shape[::-1], BF16),
            pltpu.VMEM((4, 16, quarter // 2), BF16),
            pltpu.VMEM((16, 16, quarter // 2), BF16),
            pltpu.VMEM((2, part_rows, quarter), BF16),
            pltpu.VMEM((8, part_rows, 2 * block), BF16),
            pltpu.VMEM((8, part_rows, 2 * block), BF16),
            pltpu.VMEM((2, part_rows, 2 * block), F32),
            pltpu.VMEM((32, part_rows, block), BF16),
            pltpu.VMEM((16, 16, wide_half), BF16),
            pltpu.VMEM((16, 16, wide_half), BF16),
            pltpu.VMEM(ids.shape, jnp.int32),
            dma((1,)), dma((4,)), dma((8,)), dma((1,)),
            dma((8,)), dma((8,)), dma((8,)), dma((8,)), dma((4,)), dma((4,)),
            dma((8,)), dma((8,)),
            dma((16,)), dma((16,)), dma((16,)), dma((16,)), dma((8,)), dma((8,)),
            dma((16,)), dma((16,)),
        ],
        compiler_params=pltpu.CompilerParams(
            collective_id=0, has_side_effects=True, vmem_limit_bytes=56 * 1024 * 1024
        ),
    )(ids, moe_input, expert_gate, expert_up, expert_down.T)
    parts = 1
    return pl.pallas_call(
        functools.partial(combine_kernel, width),
        out_shape=jax.ShapeDtypeStruct((rows, model), BF16),
        grid=(parts,),
        in_specs=[
            pl.BlockSpec(ids.shape, lambda i: (0, 0)),
            pl.BlockSpec(weights.shape, lambda i: (0, 0)),
            pl.BlockSpec((16 // parts, 16, wide_half), lambda i: (i, 0, 0)),
        ],
        out_specs=pl.BlockSpec((rows, model // parts), lambda i: (0, i)),
    )(ids, weights, returned)


def from_partner(block, axis, stride):
    count = lax.axis_size(axis)
    route = []
    for low in range(count):
        high = low | 1 << stride
        if high != low and high < count:
            route += [(low, high), (high, low)]
    return lax.ppermute(block, axis, route)


def shards(moe_input, expert_ids, route_weights, expert_gate, expert_up, expert_down):
    wide_count = lax.axis_size("wide")
    narrow_count = lax.axis_size("narrow")
    hosted = wide_count // GROUP
    row_count = moe_input.shape[0]
    quarter = moe_input.shape[1] // GROUP
    hidden_width = expert_gate.shape[1]
    out_cols = expert_down.shape[1]
    matches = expert_ids[:, :, None] == jnp.arange(hosted, dtype=jnp.int32)[None, None, :]
    routed = jnp.any(matches, axis=1).astype(jnp.int32)
    route_gain = jnp.sum(jnp.where(matches, route_weights[:, :, None], 0.0), axis=1)
    slot_rank = jnp.cumsum(routed, axis=0) - routed
    selector = (slot_rank.T[:, None, :] == jnp.arange(CAP, dtype=jnp.int32)[None, :, None]) & (
        routed.T[:, None, :] > 0
    )
    quarters = moe_input.reshape(row_count, GROUP, quarter)
    outgoing = jnp.einsum(
        "ecr,rqd->eqcd", selector.astype(jnp.bfloat16), quarters, preferred_element_type=jnp.float32
    )
    outgoing = outgoing.astype(jnp.bfloat16).reshape(hosted * GROUP, CAP, quarter)
    arrived = lax.all_to_all(outgoing, "wide", split_axis=0, concat_axis=1, tiled=True).reshape(
        wide_count * CAP, quarter
    )
    segment = lax.all_gather(arrived, "narrow", axis=0, tiled=True)
    gate_part = jnp.dot(segment, expert_gate, preferred_element_type=jnp.float32)
    up_part = jnp.dot(segment, expert_up, preferred_element_type=jnp.float32)
    partial_sums = jnp.concatenate([gate_part, up_part], axis=1)
    summed = partial_sums
    for level in range(2):
        summed = summed + from_partner(summed, "wide", level)
    hidden = (jax.nn.silu(summed[:, :hidden_width]) * summed[:, hidden_width:]).astype(jnp.bfloat16)
    expert_out = jnp.dot(
        lax.all_gather(hidden, "narrow", axis=1, tiled=True),
        expert_down,
        preferred_element_type=jnp.float32,
    ).astype(jnp.bfloat16)
    sectioned = expert_out.reshape(narrow_count, wide_count, CAP, 1, out_cols)
    returned = lax.all_to_all(
        lax.all_to_all(sectioned, "wide", split_axis=1, concat_axis=3, tiled=True),
        "narrow",
        split_axis=0,
        concat_axis=4,
        tiled=True,
    )
    returned = returned.reshape(CAP, hosted, GROUP * quarter)
    weighted = selector.astype(jnp.float32) * route_gain.T[:, None, :]
    combined = jnp.einsum(
        "ecr,ced->rd", weighted, returned.astype(jnp.float32), precision=lax.Precision.HIGHEST
    )
    return combined.astype(jnp.bfloat16)


def solution(mesh):
    in_specs = (
        P(("grp", "wide", "narrow"), None),
        P(("grp", "wide", "narrow"), None),
        P(("grp", "wide", "narrow"), None),
        P("wide", "narrow"),
        P("wide", "narrow"),
        P(None, ("wide", "narrow")),
    )
    out_specs = P(("grp", "wide", "narrow"), None)
    single = mesh.shape["wide"] == GROUP and mesh.shape["narrow"] == 4
    per_device = grouped if single else shards
    return jax.shard_map(per_device, mesh=mesh, in_specs=in_specs, out_specs=out_specs, check_vma=False)
```

```python
import functools

import jax
import jax.numpy as jnp
from jax import lax
from jax.experimental import pallas as pl
from jax.experimental.pallas import tpu as pltpu
from jax.sharding import PartitionSpec as P

GROUP = 4
CAP = 8
MESH = pl.DeviceIdType.MESH
F32 = jnp.float32
BF16 = jnp.bfloat16
BOTH_ROWS = False
BOTH_HIDDEN = True


def slot_rows(ids):
    rows = ids.shape[1]
    routed = jnp.sum(jnp.where(ids == 0, 1.0, 0.0), axis=0, keepdims=True)
    routed = jnp.broadcast_to(routed, (16, rows))
    before = lax.broadcasted_iota(jnp.int32, (rows, rows), 0) < lax.broadcasted_iota(jnp.int32, (rows, rows), 1)
    rank = jnp.dot(routed.astype(BF16), before.astype(F32).astype(BF16), preferred_element_type=F32)
    slot = lax.broadcasted_iota(jnp.int32, (16, rows), 0)
    slot = jnp.where(slot >= CAP, slot - CAP, slot).astype(F32)
    return jnp.where((rank == slot) & (routed > 0.5), 1.0, 0.0).astype(BF16)


def expert_kernel(
    ids_hbm, x_hbm, gate_hbm, up_hbm, down_hbm, ret_ref,
    x_v, gu_v, down_v, xq, seg, lhs, pbuf, rs, own, hid, obuf, ret, ids_v,
    ids_sem, x_sem, gu_sem, down_sem,
    a_send, a_recv, b_send, b_recv, c_send, c_recv,
    r_send, r_recv,
    ha_send, ha_recv, hb_send, hb_recv, hc_send, hc_recv,
    o_send, o_recv,
):
    w = lax.axis_index("wide")
    n = lax.axis_index("narrow")
    me = w * 4 + n
    mate = n + 1 - 2 * lax.rem(n, 2)
    across = lax.rem(n + 2, 4)
    diag = lax.rem(mate + 2, 4)
    quarter = gate_hbm.shape[0]
    half = quarter // 2
    block = gate_hbm.shape[1] // 4
    rows = 2 * lhs.shape[1]

    def ahead(k):
        return lax.rem(w + k, 4)

    def behind(k):
        return lax.rem(w + 4 - k, 4)

    barrier = pltpu.get_barrier_semaphore()
    for device in [{"wide": ahead(k)} for k in (2, 1, 3)] + [{"narrow": m} for m in (across, diag, mate)]:
        pl.semaphore_signal(barrier, inc=1, device_id=device, device_id_type=MESH)

    load_ids = pltpu.make_async_copy(ids_hbm, ids_v, ids_sem.at[0])
    load_ids.start()
    loads_x = []
    for k in (2, 1, 3, 0):
        cols = pl.ds(pl.multiple_of(ahead(k) * quarter, 128), quarter)
        loads_x.append(pltpu.make_async_copy(x_hbm.at[:, cols], x_v.at[k], x_sem.at[k]))
    for copy in loads_x:
        copy.start()
    loads_gu = []
    for j in range(4):
        for half_no, src in ((0, gate_hbm), (1, up_hbm)):
            loads_gu.append(
                pltpu.make_async_copy(
                    src.at[:, pl.ds(j * block, block)],
                    gu_v.at[:, pl.ds((2 * j + half_no) * block, block)],
                    gu_sem.at[2 * j + half_no],
                )
            )
    for copy in loads_gu:
        copy.start()
    load_down = pltpu.make_async_copy(down_hbm, down_v, down_sem.at[0])
    load_down.start()

    load_ids.wait()
    pick = slot_rows(ids_v[...])

    def gathered(k):
        first = jnp.dot(pick, x_v[k, :, :half], preferred_element_type=F32)
        second = jnp.dot(pick, x_v[k, :, half:], preferred_element_type=F32)
        return jnp.concatenate([first[:CAP], second[CAP:]], axis=0).astype(BF16)

    pl.semaphore_wait(barrier, 6)

    def remote(src, dst, send, recv, device):
        return pltpu.make_async_remote_copy(
            src_ref=src, dst_ref=dst, send_sem=send, recv_sem=recv, device_id=device, device_id_type=MESH
        )

    started = []

    def go(copy):
        copy.start()
        started.append(copy)
        return copy

    class Spread:
        def __init__(self, buf, place, sems, base, both):
            self.buf, self.place, self.base, self.both = buf, place, base, both
            self.a_s, self.a_r, self.b_s, self.b_r, self.c_s, self.c_r = sems
            self.mine = buf.at[place(w, n)]
            self.near, self.cross, self.close, self.far = {}, {}, {}, {}

        def send_near(self, k, source):
            i = 2 * (self.base + k)
            self.near[k] = go(remote(source, self.mine, self.a_s.at[i], self.a_r.at[i], {"wide": ahead(k)}))

        def send_cross(self, k, source):
            if self.both:
                i = 2 * (self.base + k) + 1
                device = {"wide": ahead(k), "narrow": across}
                self.cross[k] = go(remote(source, self.mine, self.a_s.at[i], self.a_r.at[i], device))

        def forward(self, k):
            if k:
                self.near[k].wait_recv()
            i = self.base + k
            ref = self.buf.at[self.place(behind(k), n)]
            if not self.both:
                self.cross[k] = go(remote(ref, ref, self.b_s.at[2 * i], self.b_r.at[2 * i], {"narrow": across}))
                self.far[k] = go(remote(ref, ref, self.c_s.at[i], self.c_r.at[i], {"narrow": diag}))
            self.close[k] = go(remote(ref, ref, self.b_s.at[2 * i + 1], self.b_r.at[2 * i + 1], {"narrow": mate}))

        def forward_cross(self, k):
            if self.both:
                self.cross[k].wait_recv()
                i = self.base + k
                ref = self.buf.at[self.place(behind(k), across)]
                self.far[k] = go(remote(ref, ref, self.c_s.at[i], self.c_r.at[i], {"narrow": mate}))

        def wait_close(self):
            for k in self.close:
                self.close[k].wait_recv()

        def wait_cross(self):
            if not self.both:
                for k in self.cross:
                    self.cross[k].wait_recv()

        def wait_far(self):
            for k in self.far:
                self.far[k].wait_recv()

    def seg_place(w_, n_):
        return (n_ // 2) * 8 + w_ * 2 + lax.rem(n_, 2)

    seg_mine = seg_place(w, n)
    spread = Spread(seg, seg_place, (a_send, a_recv, b_send, b_recv, c_send, c_recv), 0, BOTH_ROWS)
    for i, k in enumerate((2, 1, 3, 0)):
        loads_x[i].wait()
        value = gathered(k)
        if k:
            xq[k] = value
            spread.send_near(k, xq.at[k])
        else:
            seg[seg_mine] = value
    for k in (2, 1, 3):
        spread.send_cross(k, xq.at[k])
    spread.send_cross(0, seg.at[seg_mine])
    for k in (0, 1, 3, 2):
        spread.forward(k)
    spread.wait_close()

    side = n // 2
    part_rows = rows // 2

    def fill(c):
        part_side = side if c == 0 else 1 - side
        part = seg[pl.ds(part_side * 8, 8)].astype(F32)
        lhs[c, :, :half] = part[:, :CAP].reshape(part_rows, half).astype(BF16)
        lhs[c, :, half:] = part[:, CAP:].reshape(part_rows, half).astype(BF16)

    r_copies = {}

    def partial_sums(c, k):
        cols = pl.ds(pl.multiple_of(ahead(k) * 2 * block, 128), 2 * block)
        value = jnp.dot(lhs[c], gu_v[:, cols], preferred_element_type=F32)
        if k:
            i = 4 * c + k
            pbuf[i] = value.astype(BF16)
            r_copies[i] = go(remote(pbuf.at[i], rs.at[i], r_send.at[i], r_recv.at[i], {"wide": ahead(k)}))
        else:
            own[c] = value

    fill(0)
    for copy in loads_gu:
        copy.wait()
    partial_sums(0, 2)
    partial_sums(0, 1)
    partial_sums(0, 3)
    partial_sums(0, 0)
    for k in (0, 1, 3, 2):
        spread.forward_cross(k)
    spread.wait_cross()
    spread.wait_far()
    fill(1)
    for k in (2, 1, 3, 0):
        partial_sums(1, k)

    h_spread = {}

    def hid_place(c):
        def place(w_, n_):
            n_side = n_ // 2
            return (n_side if c == 0 else 1 - n_side) * 16 + n_ * 4 + w_

        return place

    for c in range(2):
        for k in (1, 3, 2):
            r_copies[4 * c + k].wait_recv()
        total = own[c]
        for k in (1, 3, 2):
            total = total + rs[4 * c + k].astype(F32)
        gate, up = total[:, :block], total[:, block:]
        place = hid_place(c)
        mine = place(w, n)
        hid[mine] = (gate / (1.0 + jnp.exp(-gate)) * up).astype(BF16)
        h_spread[c] = Spread(
            hid, place, (ha_send, ha_recv, hb_send, hb_recv, hc_send, hc_recv), 4 * c, BOTH_HIDDEN
        )
        for k in (2, 1, 3):
            h_spread[c].send_near(k, hid.at[mine])
        for k in (2, 1, 3, 0):
            h_spread[c].send_cross(k, hid.at[mine])
        h_spread[c].forward(0)
    for c in range(2):
        for k in (1, 3, 2):
            h_spread[c].forward(k)
        for k in (0, 1, 3, 2):
            h_spread[c].forward_cross(k)
    load_down.wait()

    def down_part(n_):
        left = jnp.concatenate(
            [
                jnp.concatenate([hid[16 * s + n_ * 4 + j] for j in range(4)], axis=1)
                for s in range(2)
            ],
            axis=0,
        )
        right = down_v[:, pl.ds(pl.multiple_of(n_ * 4 * block, 128), 4 * block)]
        return lax.dot_general(left, right, (((1,), (1,)), ((), ())), preferred_element_type=F32)

    out = down_part(n)
    for c in range(2):
        h_spread[c].wait_close()
    out = out + down_part(mate)
    for c in range(2):
        h_spread[c].wait_cross()
    out = out + down_part(across)
    for c in range(2):
        h_spread[c].wait_far()
    out = out + down_part(diag)

    width = out.shape[1]
    wide_half = obuf.shape[2]
    first = out[:, :wide_half].reshape(16, CAP, wide_half)
    second = jnp.concatenate(
        [out[:, wide_half:], jnp.zeros((rows, 2 * wide_half - width), F32)], axis=1
    ).reshape(16, CAP, wide_half)
    obuf[...] = jnp.concatenate([first, second], axis=1).astype(BF16)
    o_copies = []
    for t in range(1, 16):
        d = lax.rem(me + t, 16)
        o_copies.append(
            go(
                remote(
                    obuf.at[seg_place(d // 4, lax.rem(d, 4))], ret.at[me], o_send.at[t], o_recv.at[t],
                    {"wide": d // 4, "narrow": lax.rem(d, 4)},
                )
            )
        )
    ret[me] = obuf[seg_mine]
    for copy in o_copies:
        copy.wait_recv()
    ret_ref[...] = ret[...]
    for copy in started:
        copy.wait_send()


def combine_kernel(width, ids_ref, weights_ref, ret_ref, out_ref):
    ids = ids_ref[...]
    rows = ids.shape[1]
    hit = ids == 0
    gain = jnp.sum(jnp.where(hit, weights_ref[...], 0.0), axis=0, keepdims=True)
    gain = jnp.transpose(jnp.broadcast_to(gain, (128, rows)))
    place = slot_rows(ids)
    place = jnp.where(lax.broadcasted_iota(jnp.int32, place.shape, 0) < CAP, place.astype(F32), 0.0).astype(BF16)
    pieces = []
    wide_half = ret_ref.shape[2]
    for j in range(ret_ref.shape[0]):
        value = ret_ref[j].astype(F32)
        pieces += [value[:CAP], value[CAP:, :width - wide_half]]
    slots = jnp.concatenate(pieces, axis=1)
    slots = jnp.concatenate([slots, jnp.zeros_like(slots)], axis=0).astype(BF16)
    placed = lax.dot_general(place, slots, (((0,), (0,)), ((), ())), preferred_element_type=F32)
    gains = jnp.concatenate([gain] * (placed.shape[1] // 128), axis=1)
    out_ref[...] = (placed * gains).astype(BF16)


def grouped(moe_input, expert_ids, route_weights, expert_gate, expert_up, expert_down):
    rows, model = moe_input.shape
    quarter, hidden = expert_gate.shape
    width = expert_down.shape[1]
    block = hidden // 4
    wide_half = -(-width // 256) * 128
    part_rows = 8 * CAP
    ids, weights = expert_ids.T, route_weights.T
    dma = pltpu.SemaphoreType.DMA
    any_spec = pl.BlockSpec(memory_space=pl.ANY)
    vmem_spec = pl.BlockSpec(memory_space=pltpu.VMEM)
    returned = pl.pallas_call(
        expert_kernel,
        out_shape=pltpu.VMEM((16, 16, wide_half), BF16),
        in_specs=[any_spec] * 5,
        out_specs=vmem_spec,
        scratch_shapes=[
            pltpu.VMEM((4, rows, quarter), BF16),
            pltpu.VMEM((quarter, 2 * hidden), BF16),
            pltpu.VMEM(expert_down.shape[::-1], BF16),
            pltpu.VMEM((4, 16, quarter // 2), BF16),
            pltpu.VMEM((16, 16, quarter // 2), BF16),
            pltpu.VMEM((2, part_rows, quarter), BF16),
            pltpu.VMEM((8, part_rows, 2 * block), BF16),
            pltpu.VMEM((8, part_rows, 2 * block), BF16),
            pltpu.VMEM((2, part_rows, 2 * block), F32),
            pltpu.VMEM((32, part_rows, block), BF16),
            pltpu.VMEM((16, 16, wide_half), BF16),
            pltpu.VMEM((16, 16, wide_half), BF16),
            pltpu.VMEM(ids.shape, jnp.int32),
            dma((1,)), dma((4,)), dma((8,)), dma((1,)),
            dma((8,)), dma((8,)), dma((8,)), dma((8,)), dma((4,)), dma((4,)),
            dma((8,)), dma((8,)),
            dma((16,)), dma((16,)), dma((16,)), dma((16,)), dma((8,)), dma((8,)),
            dma((16,)), dma((16,)),
        ],
        compiler_params=pltpu.CompilerParams(
            collective_id=0, has_side_effects=True, vmem_limit_bytes=56 * 1024 * 1024
        ),
    )(ids, moe_input, expert_gate, expert_up, expert_down.T)
    parts = 1
    return pl.pallas_call(
        functools.partial(combine_kernel, width),
        out_shape=jax.ShapeDtypeStruct((rows, model), BF16),
        grid=(parts,),
        in_specs=[
            pl.BlockSpec(ids.shape, lambda i: (0, 0)),
            pl.BlockSpec(weights.shape, lambda i: (0, 0)),
            pl.BlockSpec(memory_space=pltpu.VMEM),
        ],
        out_specs=pl.BlockSpec((rows, model // parts), lambda i: (0, i)),
    )(ids, weights, returned)


def from_partner(block, axis, stride):
    count = lax.axis_size(axis)
    route = []
    for low in range(count):
        high = low | 1 << stride
        if high != low and high < count:
            route += [(low, high), (high, low)]
    return lax.ppermute(block, axis, route)


def shards(moe_input, expert_ids, route_weights, expert_gate, expert_up, expert_down):
    wide_count = lax.axis_size("wide")
    narrow_count = lax.axis_size("narrow")
    hosted = wide_count // GROUP
    row_count = moe_input.shape[0]
    quarter = moe_input.shape[1] // GROUP
    hidden_width = expert_gate.shape[1]
    out_cols = expert_down.shape[1]
    matches = expert_ids[:, :, None] == jnp.arange(hosted, dtype=jnp.int32)[None, None, :]
    routed = jnp.any(matches, axis=1).astype(jnp.int32)
    route_gain = jnp.sum(jnp.where(matches, route_weights[:, :, None], 0.0), axis=1)
    slot_rank = jnp.cumsum(routed, axis=0) - routed
    selector = (slot_rank.T[:, None, :] == jnp.arange(CAP, dtype=jnp.int32)[None, :, None]) & (
        routed.T[:, None, :] > 0
    )
    quarters = moe_input.reshape(row_count, GROUP, quarter)
    outgoing = jnp.einsum(
        "ecr,rqd->eqcd", selector.astype(jnp.bfloat16), quarters, preferred_element_type=jnp.float32
    )
    outgoing = outgoing.astype(jnp.bfloat16).reshape(hosted * GROUP, CAP, quarter)
    arrived = lax.all_to_all(outgoing, "wide", split_axis=0, concat_axis=1, tiled=True).reshape(
        wide_count * CAP, quarter
    )
    segment = lax.all_gather(arrived, "narrow", axis=0, tiled=True)
    gate_part = jnp.dot(segment, expert_gate, preferred_element_type=jnp.float32)
    up_part = jnp.dot(segment, expert_up, preferred_element_type=jnp.float32)
    partial_sums = jnp.concatenate([gate_part, up_part], axis=1)
    summed = partial_sums
    for level in range(2):
        summed = summed + from_partner(summed, "wide", level)
    hidden = (jax.nn.silu(summed[:, :hidden_width]) * summed[:, hidden_width:]).astype(jnp.bfloat16)
    expert_out = jnp.dot(
        lax.all_gather(hidden, "narrow", axis=1, tiled=True),
        expert_down,
        preferred_element_type=jnp.float32,
    ).astype(jnp.bfloat16)
    sectioned = expert_out.reshape(narrow_count, wide_count, CAP, 1, out_cols)
    returned = lax.all_to_all(
        lax.all_to_all(sectioned, "wide", split_axis=1, concat_axis=3, tiled=True),
        "narrow",
        split_axis=0,
        concat_axis=4,
        tiled=True,
    )
    returned = returned.reshape(CAP, hosted, GROUP * quarter)
    weighted = selector.astype(jnp.float32) * route_gain.T[:, None, :]
    combined = jnp.einsum(
        "ecr,ced->rd", weighted, returned.astype(jnp.float32), precision=lax.Precision.HIGHEST
    )
    return combined.astype(jnp.bfloat16)


def solution(mesh):
    in_specs = (
        P(("grp", "wide", "narrow"), None),
        P(("grp", "wide", "narrow"), None),
        P(("grp", "wide", "narrow"), None),
        P("wide", "narrow"),
        P("wide", "narrow"),
        P(None, ("wide", "narrow")),
    )
    out_specs = P(("grp", "wide", "narrow"), None)
    single = mesh.shape["wide"] == GROUP and mesh.shape["narrow"] == 4
    per_device = grouped if single else shards
    return jax.shard_map(per_device, mesh=mesh, in_specs=in_specs, out_specs=out_specs, check_vma=False)
```
